32 devices in a mesh: occ: 8 (over z, y), aux: 4 (over x, core).
Axes of the slice: x: 2, y: 2, z: 4, core: 2. Of those that a mesh axis runs over, the one named last changes fastest.
Arguments:
- factors: bfloat16 [2048, 16, 1024], P('aux', 'occ'), may hold values from -32 to 32
- partner: bfloat16 [2048, 1024], P('aux', 'occ'), may hold values from -0.09375 to 0.09375
- occupied_energy: float32 [16], P('occ'), may hold values from -2 to -0.5
- partner_energy: float32 [1], replicated, may hold values from -3 to -0.3
- virtual_energy: float32 [1024], replicated, may hold values from 0.2 to 3
Outputs:
- amplitudes: bfloat16 [16384, 1024], P(('occ', 'aux'))
- density_factors: bfloat16 [2048, 16, 1024], P('aux', 'occ')
The draws below stay inside these ranges and needn't reach their ends.
All inputs are finite; a program needn't handle non-finite values.
Results may differ from the reference program's by a relative error of at most 0.015.
Values may be sent and summed in bfloat16 or wider, within the bound.
No kernel may reach another device: no remote copies, remote signals or barrier semaphores. Data moves between devices by JAX's collectives and lax.ppermute only.
A program may use at most 64 MiB of HBM per device.

```python
import jax
import jax.numpy as jnp
from jax import lax

V = 1024
Q_DEV = 512
OCC = 16
Q = 2048
N_AUX = 4


def levels(key, shape, shards, low, high):
    def one(position, shards_of):
        draws = jax.random.uniform(jax.random.fold_in(jax.random.fold_in(key, 6), position), (shards_of,), jnp.float32, low / len(shards), high / len(shards))
        return jnp.repeat(jnp.exp(draws), shape[position] // shards_of).reshape((-1,) + (1,) * (len(shape) - position - 1))

    loudness = one(*shards[0])
    for cut in shards[1:]:
        loudness = loudness * one(*cut)
    return loudness


def bell_draw(rng, dims, spread, reach, cuts=(), held_as=jnp.bfloat16):
    gain = levels(rng, dims, cuts, -0.22, 0.18) if cuts else 1.0
    entries = jax.random.normal(rng, dims, jnp.float32) * spread * gain
    return jnp.minimum(jnp.maximum(entries, -reach), reach).astype(held_as)


def setup_inputs(seed: int = 0) -> dict:
    key_of = jax.random.split(jax.random.key(seed), 6)
    return {
        "factors": bell_draw(key_of[0], (Q, OCC, V), (8 * (V / Q) ** 0.5), 32.0, ((0, 4), (1, 8))),
        "partner": bell_draw(key_of[1], (Q, V), (0.5 / V ** 0.5), 0.09375, ((0, 4), (1, 8))),
        "occupied_energy": jnp.clip(-2.0 + 1.5 * jax.random.uniform(key_of[2], (OCC,), jnp.float32) ** levels(key_of[2], (OCC,), ((0, 8),), -0.2, 0.2), -2.0, -0.5),
        "partner_energy": jnp.clip(jax.random.uniform(key_of[3], (1,), jnp.float32, -3.0, -0.3), -3.0, -0.3),
        "virtual_energy": jnp.clip(jax.random.uniform(key_of[4], (V,), jnp.float32, 0.2, 3.0), 0.2, 3.0),
    }


def reference(factors, partner, occupied_energy, partner_energy, virtual_energy):
    occ_total = factors.shape[1]
    virt_count = factors.shape[2]
    factor_blocks = factors.reshape(N_AUX, Q_DEV, occ_total * virt_count)
    partner_blocks = partner.reshape(N_AUX, Q_DEV, virt_count)

    def add_block(carry, pieces):
        block_rows, block_cols = pieces
        partial_sum = lax.dot_general(block_rows.astype(jnp.float32), block_cols.astype(jnp.float32), (((0,), (0,)), ((), ())), precision=lax.Precision.HIGHEST)
        rounded = lax.optimization_barrier(partial_sum.astype(jnp.bfloat16))
        return carry + rounded.astype(jnp.float32), None

    start_sum = jnp.zeros((occ_total * virt_count, virt_count), jnp.float32)
    integrals, _ = lax.scan(add_block, start_sum, (factor_blocks, partner_blocks))
    occ_rows = jnp.repeat(occupied_energy, virt_count)
    virt_rows = jnp.tile(virtual_energy, occ_total)
    divisor = virt_rows[:, None] + virtual_energy[None, :] - occ_rows[:, None] - partner_energy[0]
    amplitudes = (-integrals / divisor).astype(jnp.bfloat16)
    amp_cube = amplitudes.reshape(occ_total, virt_count, virt_count)
    partner_wide = partner.astype(jnp.float32)

    def one_orbital(amp_block):
        block_wide = amp_block.astype(jnp.float32)
        direct = jnp.dot(partner_wide, block_wide.T, precision=lax.Precision.HIGHEST)
        swapped = jnp.dot(partner_wide, block_wide, precision=lax.Precision.HIGHEST)
        return (2.0 * direct - swapped).astype(jnp.bfloat16)

    density = lax.map(one_orbital, amp_cube)
    return amplitudes, jnp.transpose(density, (1, 0, 2))
```

```python
import jax
import jax.numpy as jnp
from jax import lax
from jax.sharding import PartitionSpec as P

BF16 = jnp.bfloat16
F32 = jnp.float32


def lookup(entries, indices):
    positions = jnp.arange(entries.shape[0], dtype=jnp.int32)
    matches = indices[:, None] == positions[None, :]
    return jnp.sum(jnp.where(matches, entries[None, :], 0.0), axis=1)


def scatter_shards(factors, partner, occupied_energy, partner_energy, virtual_energy):
    aux_rows, local_occ, virt_count = factors.shape
    partner_full = lax.all_gather(partner, "occ", axis=1, tiled=True)
    flat_factors = factors.reshape(aux_rows, local_occ * virt_count)
    total_rows = local_occ * virt_count
    row_share = total_rows // lax.axis_size("aux")
    own_first = lax.axis_index("aux") * row_share
    integrals = lax.psum_scatter(
        lax.dot_general(flat_factors, partner_full, (((0,), (0,)), ((), ())), preferred_element_type=F32).astype(BF16),
        "aux",
        scatter_dimension=0,
        tiled=True,
    ).astype(F32)
    row_ids = own_first + jnp.arange(row_share, dtype=jnp.int32)
    occ_part = lookup(occupied_energy, row_ids // virt_count)
    virt_part = lookup(virtual_energy, row_ids % virt_count)
    divisor = virt_part[:, None] + virtual_energy[None, :] - occ_part[:, None] - partner_energy[0]
    amp_shard = (-integrals / divisor).astype(BF16)
    amp_full = lax.all_gather(amp_shard, "aux", axis=0, tiled=True)
    amp_cube = amp_full.reshape(local_occ, virt_count, virt_count)
    direct = jnp.einsum("qb,iab->qia", partner_full, amp_cube, preferred_element_type=F32)
    swapped = jnp.einsum("qb,iba->qia", partner_full, amp_cube, preferred_element_type=F32)
    density = (2.0 * direct - swapped).astype(BF16)
    return (amp_shard, density)


def pair_shards(factors, partner, occupied_energy, partner_energy, virtual_energy):
    aux_rows, local_occ, virt_count = factors.shape
    n_aux = lax.axis_size("aux")
    n_occ = lax.axis_size("occ")
    share = local_occ * virt_count // n_aux
    per_occ = virt_count // share
    across = [(d, (d + n_aux // 2) % n_aux) for d in range(n_aux)]
    within = [(d, d ^ 1) for d in range(n_aux)]

    flat = factors.reshape(aux_rows, local_occ * virt_count)
    pieces = [flat[:, p * share : (p + 1) * share] for p in range(n_aux)]

    shard = partner.T
    shard = jnp.concatenate([shard, lax.ppermute(shard, "aux", across)], axis=1)
    blocks = {0: shard}
    for k in range(2, n_occ, 2):
        blocks[k] = lax.ppermute(shard, "occ", [(d, d ^ k) for d in range(n_occ)])
    for k in range(0, n_occ, 2):
        blocks[k + 1] = lax.ppermute(blocks[k], "occ", [(d, d ^ 1) for d in range(n_occ)])
    here = lax.axis_index("occ")
    gathered = jnp.zeros((n_occ,) + shard.shape, BF16)
    for k, block in blocks.items():
        gathered = lax.dynamic_update_index_in_dim(gathered, block, here ^ k, 0)
    gathered = gathered.reshape(virt_count, 2 * aux_rows)
    own_t, far_t = gathered[:, :aux_rows], gathered[:, aux_rows:]
    own = own_t.T

    fetched = [lax.ppermute(piece, "aux", across) for piece in pieces]
    amps = []
    for p in range(n_aux):
        part = jnp.dot(own_t, pieces[p], preferred_element_type=F32)
        part = part + jnp.dot(far_t, fetched[p], preferred_element_type=F32)
        part = part.astype(BF16)
        other = lax.ppermute(part, "aux", within)
        integrals = part.astype(F32) + other.astype(F32)
        i, first = p // per_occ, (p % per_occ) * share
        columns = virtual_energy[first : first + share] - occupied_energy[i] - partner_energy[0]
        amps.append((-integrals / (virtual_energy[:, None] + columns[None, :])).astype(BF16))

    density = []
    for i in range(local_occ):
        amp = jnp.concatenate(amps[i * per_occ : (i + 1) * per_occ], axis=1)
        direct = jnp.dot(own, amp, preferred_element_type=F32)
        swapped = lax.dot_general(own, amp, (((1,), (1,)), ((), ())), preferred_element_type=F32)
        density.append((2.0 * direct - swapped).astype(BF16))
    amp_shard = lax.dynamic_index_in_dim(jnp.stack(amps), lax.axis_index("aux"), 0, keepdims=False).T
    return (amp_shard, jnp.stack(density, axis=1))


def solution(mesh):
    n_aux, n_occ = mesh.shape["aux"], mesh.shape["occ"]
    fetch = n_aux == 2 * 2 and n_occ & (n_occ - 1) == 0
    return jax.shard_map(
        pair_shards if fetch else scatter_shards,
        mesh=mesh,
        in_specs=(P("aux", "occ", None), P("aux", "occ"), P("occ"), P(), P()),
        out_specs=(P(("occ", "aux"), None), P("aux", "occ", None)),
        check_vma=False,
    )
```

```python
import jax
import jax.numpy as jnp
from jax import lax
from jax.sharding import PartitionSpec as P

BF16 = jnp.bfloat16
F32 = jnp.float32


def lookup(entries, indices):
    positions = jnp.arange(entries.shape[0], dtype=jnp.int32)
    matches = indices[:, None] == positions[None, :]
    return jnp.sum(jnp.where(matches, entries[None, :], 0.0), axis=1)


def scatter_shards(factors, partner, occupied_energy, partner_energy, virtual_energy):
    aux_rows, local_occ, virt_count = factors.shape
    partner_full = lax.all_gather(partner, "occ", axis=1, tiled=True)
    flat_factors = factors.reshape(aux_rows, local_occ * virt_count)
    total_rows = local_occ * virt_count
    row_share = total_rows // lax.axis_size("aux")
    own_first = lax.axis_index("aux") * row_share
    integrals = lax.psum_scatter(
        lax.dot_general(flat_factors, partner_full, (((0,), (0,)), ((), ())), preferred_element_type=F32).astype(BF16),
        "aux",
        scatter_dimension=0,
        tiled=True,
    ).astype(F32)
    row_ids = own_first + jnp.arange(row_share, dtype=jnp.int32)
    occ_part = lookup(occupied_energy, row_ids // virt_count)
    virt_part = lookup(virtual_energy, row_ids % virt_count)
    divisor = virt_part[:, None] + virtual_energy[None, :] - occ_part[:, None] - partner_energy[0]
    amp_shard = (-integrals / divisor).astype(BF16)
    amp_full = lax.all_gather(amp_shard, "aux", axis=0, tiled=True)
    amp_cube = amp_full.reshape(local_occ, virt_count, virt_count)
    direct = jnp.einsum("qb,iab->qia", partner_full, amp_cube, preferred_element_type=F32)
    swapped = jnp.einsum("qb,iba->qia", partner_full, amp_cube, preferred_element_type=F32)
    density = (2.0 * direct - swapped).astype(BF16)
    return (amp_shard, density)


def after(value, *others):
    return lax.optimization_barrier((value,) + others)[0]


def pair_shards(factors, partner, occupied_energy, partner_energy, virtual_energy):
    aux_rows, local_occ, virt_count = factors.shape
    n_aux = lax.axis_size("aux")
    n_occ = lax.axis_size("occ")
    share = local_occ * virt_count // n_aux
    per_occ = virt_count // share
    across = [(d, (d + n_aux // 2) % n_aux) for d in range(n_aux)]
    within = [(d, d ^ 1) for d in range(n_aux)]

    def occ_swap(value, k):
        return lax.ppermute(value, "occ", [(d, d ^ k) for d in range(n_occ)])

    def piece_of(source, p):
        i, first = p // per_occ, (p % per_occ) * share
        return source[:, i, first : first + share]

    far = lax.ppermute(partner, "aux", across)
    pieces = [piece_of(factors, p) for p in range(2)]
    fetched = [lax.ppermute(piece, "aux", across) for piece in pieces]

    blocks = {0: jnp.stack([partner.T, far.T])}
    step = 2
    while step < n_occ:
        for k in range(0, step, 2):
            blocks[k + step] = occ_swap(blocks[k], step)
        step *= 2
    for k in range(0, n_occ, 2):
        blocks[k + 1] = occ_swap(blocks[k], 1)

    later = after(factors, blocks[0])
    for p in range(2, n_aux):
        pieces.append(piece_of(later, p))
        fetched.append(lax.ppermute(after(pieces[p], fetched[p - 2]), "aux", across))

    here = lax.axis_index("occ")
    own_t = jnp.zeros((n_occ,) + partner.T.shape, BF16)
    far_t = own_t
    for k, block in blocks.items():
        own_t = lax.dynamic_update_index_in_dim(own_t, block[0], here ^ k, 0)
        far_t = lax.dynamic_update_index_in_dim(far_t, block[1], here ^ k, 0)
    own_t = own_t.reshape(virt_count, aux_rows)
    far_t = far_t.reshape(virt_count, aux_rows)

    columns = virtual_energy[None, :] - occupied_energy[:, None] - partner_energy[0]
    columns, rows = lax.optimization_barrier((columns, virtual_energy))

    amps = []
    for p in range(n_aux):
        part = jnp.dot(own_t, pieces[p], preferred_element_type=F32)
        part = part + jnp.dot(far_t, fetched[p], preferred_element_type=F32)
        part = part.astype(BF16)
        other = lax.ppermute(part, "aux", within)
        part, other, row, column = lax.optimization_barrier((part, other, rows, columns))
        i, first = p // per_occ, (p % per_occ) * share
        integrals = part.astype(F32) + other.astype(F32)
        amps.append((-integrals / (row[:, None] + column[i, None, first : first + share])).astype(BF16))

    density = []
    for i in range(local_occ):
        amp = jnp.concatenate(amps[i * per_occ : (i + 1) * per_occ], axis=1)
        direct = lax.dot_general(own_t, amp, (((0,), (0,)), ((), ())), preferred_element_type=F32)
        swapped = lax.dot_general(own_t, amp, (((0,), (1,)), ((), ())), preferred_element_type=F32)
        density.append((2.0 * direct - swapped).astype(BF16))
    amp_shard = amps[0]
    for p in range(1, n_aux):
        amp_shard = jnp.where(lax.axis_index("aux") == p, amps[p], amp_shard)
    return (amp_shard.T, jnp.stack(density, axis=1))


def solution(mesh):
    n_aux, n_occ = mesh.shape["aux"], mesh.shape["occ"]
    fetch = n_aux == 2 * 2 and n_occ & (n_occ - 1) == 0
    return jax.shard_map(
        pair_shards if fetch else scatter_shards,
        mesh=mesh,
        in_specs=(P("aux", "occ", None), P("aux", "occ"), P("occ"), P(), P()),
        out_specs=(P(("occ", "aux"), None), P("aux", "occ", None)),
        check_vma=False,
    )
```

```python
import jax
import jax.numpy as jnp
from jax import lax
from jax.experimental import pallas as pl
from jax.experimental.pallas import tpu as pltpu
from jax.sharding import PartitionSpec as P

BF16 = jnp.bfloat16
F32 = jnp.float32


def lookup(entries, indices):
    positions = jnp.arange(entries.shape[0], dtype=jnp.int32)
    matches = indices[:, None] == positions[None, :]
    return jnp.sum(jnp.where(matches, entries[None, :], 0.0), axis=1)


def scatter_shards(factors, partner, occupied_energy, partner_energy, virtual_energy):
    aux_rows, local_occ, virt_count = factors.shape
    partner_full = lax.all_gather(partner, "occ", axis=1, tiled=True)
    flat_factors = factors.reshape(aux_rows, local_occ * virt_count)
    total_rows = local_occ * virt_count
    row_share = total_rows // lax.axis_size("aux")
    own_first = lax.axis_index("aux") * row_share
    integrals = lax.psum_scatter(
        lax.dot_general(flat_factors, partner_full, (((0,), (0,)), ((), ())), preferred_element_type=F32).astype(BF16),
        "aux",
        scatter_dimension=0,
        tiled=True,
    ).astype(F32)
    row_ids = own_first + jnp.arange(row_share, dtype=jnp.int32)
    occ_part = lookup(occupied_energy, row_ids // virt_count)
    virt_part = lookup(virtual_energy, row_ids % virt_count)
    divisor = virt_part[:, None] + virtual_energy[None, :] - occ_part[:, None] - partner_energy[0]
    amp_shard = (-integrals / divisor).astype(BF16)
    amp_full = lax.all_gather(amp_shard, "aux", axis=0, tiled=True)
    amp_cube = amp_full.reshape(local_occ, virt_count, virt_count)
    direct = jnp.einsum("qb,iab->qia", partner_full, amp_cube, preferred_element_type=F32)
    swapped = jnp.einsum("qb,iba->qia", partner_full, amp_cube, preferred_element_type=F32)
    density = (2.0 * direct - swapped).astype(BF16)
    return (amp_shard, density)


def after(value, *others):
    return lax.optimization_barrier((value,) + others)[0]


def cost(flops, *arrays):
    moved = sum(a.size * a.dtype.itemsize for a in arrays)
    return pl.CostEstimate(flops=flops, bytes_accessed=moved, transcendentals=0)


def shaped(shape, dtype=BF16):
    return jax.ShapeDtypeStruct(shape, dtype)


def split_factors(factors, near):
    aux_rows, local_occ, virt_count = factors.shape
    half, rows = virt_count // 2, aux_rows // 8

    def body(near_ref, f_ref, *out_refs):
        first, second = f_ref[:, 0, :], f_ref[:, 1, :]
        swap = near_ref[0] == 1
        kept = jnp.where(swap, second, first)
        sent = jnp.where(swap, first, second)
        for at, value in enumerate((kept, sent)):
            for h in range(2):
                out_refs[2 * at + h][...] = value[:, h * half : (h + 1) * half]

    out = shaped((aux_rows, half))
    return pl.pallas_call(
        body,
        grid=(aux_rows // rows,),
        in_specs=[pl.BlockSpec(memory_space=pltpu.SMEM), pl.BlockSpec((rows, local_occ, virt_count), lambda r: (r, 0, 0))],
        out_specs=[pl.BlockSpec((rows, half), lambda r: (r, 0))] * 4,
        out_shape=[out] * 4,
        cost_estimate=cost(0, factors, factors),
        name="split_factors",
    )(near, factors)


def amplitudes_of(part, other, row, column):
    wide = jnp.concatenate([row] * (part.shape[1] // row.shape[1]), axis=1)
    integrals = part.astype(F32) + other.astype(F32)
    return (-integrals / (wide + column)).astype(BF16)


def amplitude_piece(part, other, rows, column):
    virt_count, share = part.shape
    block = virt_count // 4

    def body(part_ref, other_ref, row_ref, column_ref, out_ref):
        out_ref[...] = amplitudes_of(part_ref[...], other_ref[...], row_ref[...], column_ref[...])

    tile = pl.BlockSpec((block, share), lambda r: (r, 0))
    return pl.pallas_call(
        body,
        grid=(virt_count // block,),
        in_specs=[
            tile,
            tile,
            pl.BlockSpec((block, rows.shape[1]), lambda r: (r, 0)),
            pl.BlockSpec((1, share), lambda r: (0, 0)),
        ],
        out_specs=tile,
        out_shape=shaped(part.shape),
        cost_estimate=cost(10 * part.size, part, part, part),
        name="amplitude_piece",
    )(part, other, rows, column)


def finish(near, part, other, rows, column, own, direct, swapped, near_density):
    virt_count, share = part.shape
    aux_rows = own.shape[0]
    block = aux_rows // 4

    def body(near_ref, part_ref, other_ref, row_ref, column_ref, own_ref, direct_ref, swapped_ref, ready_ref, out_ref, amp_ref):
        @pl.when(pl.program_id(0) == 0)
        def _():
            amp_ref[...] = amplitudes_of(part_ref[...], other_ref[...], row_ref[...], column_ref[...])

        own_rows = own_ref[...]
        amp = amp_ref[...]
        last_direct = 2.0 * jnp.dot(own_rows, amp, preferred_element_type=F32)
        last_swapped = lax.dot_general(own_rows[:, virt_count - share :], amp, (((1,), (1,)), ((), ())), preferred_element_type=F32)
        density = jnp.concatenate([direct_ref[...], last_direct], axis=1) - (swapped_ref[...] + last_swapped)
        density = density.astype(BF16)
        ready = ready_ref[...]
        swap = near_ref[0] == 1
        out_ref[:, 0, :] = jnp.where(swap, density, ready)
        out_ref[:, 1, :] = jnp.where(swap, ready, density)

    whole = lambda r: (0, 0)
    band = lambda r: (r, 0)
    return pl.pallas_call(
        body,
        grid=(aux_rows // block,),
        in_specs=[
            pl.BlockSpec(memory_space=pltpu.SMEM),
            pl.BlockSpec(part.shape, whole),
            pl.BlockSpec(other.shape, whole),
            pl.BlockSpec(rows.shape, whole),
            pl.BlockSpec((1, share), whole),
            pl.BlockSpec((block, virt_count), band),
            pl.BlockSpec((block, virt_count - share), band),
            pl.BlockSpec((block, virt_count), band),
            pl.BlockSpec((block, virt_count), band),
        ],
        out_specs=pl.BlockSpec((block, 2, virt_count), lambda r: (r, 0, 0)),
        out_shape=shaped((aux_rows, 2, virt_count)),
        scratch_shapes=[pltpu.VMEM(part.shape, BF16)],
        compiler_params=pltpu.CompilerParams(vmem_limit_bytes=32 * 1024 * 1024),
        cost_estimate=cost(4 * aux_rows * virt_count * share, part, other, own, swapped, near_density, near_density),
        name="finish_density",
    )(near, part, other, rows, column, own, direct, swapped, near_density)


def pair_shards(factors, partner, occupied_energy, partner_energy, virtual_energy):
    aux_rows, local_occ, virt_count = factors.shape
    n_aux = lax.axis_size("aux")
    n_occ = lax.axis_size("occ")
    half = virt_count // 2
    across = [(d, (d + n_aux // 2) % n_aux) for d in range(n_aux)]
    within = [(d, d ^ 1) for d in range(n_aux)]
    place = lax.axis_index("aux")
    near, core = place // 2, place % 2
    near_arr = near.astype(jnp.int32).reshape(1)

    def occ_swap(value, k):
        return lax.ppermute(value, "occ", [(d, d ^ k) for d in range(n_occ)])

    shard = partner.T
    far_shard = lax.ppermute(shard, "aux", across)
    kept_sent = split_factors(factors, near_arr)
    kept, sent = kept_sent, kept_sent[2:] + kept_sent[:2]
    fetched = [lax.ppermute(piece, "aux", across) for piece in sent[:2]]

    blocks = {0: jnp.stack([shard, far_shard])}
    step = n_occ // 2
    while step > 1:
        for k in sorted(blocks):
            blocks[k + step] = occ_swap(blocks[k], step)
        step //= 2
    for k in sorted(blocks):
        blocks[k + 1] = occ_swap(blocks[k], 1)

    for p in range(2, 4):
        fetched.append(lax.ppermute(after(sent[p], fetched[p - 2]), "aux", across))

    here = lax.axis_index("occ")
    own_t = jnp.zeros((n_occ,) + shard.shape, BF16)
    far_t = own_t
    for k, block in blocks.items():
        own_t = lax.dynamic_update_index_in_dim(own_t, block[0], here ^ k, 0)
        far_t = lax.dynamic_update_index_in_dim(far_t, block[1], here ^ k, 0)
    own_t = own_t.reshape(virt_count, aux_rows)
    far_t = far_t.reshape(virt_count, aux_rows)
    own = after(own_t.T)

    energies = virtual_energy[None, :] - occupied_energy[:, None] - partner_energy[0]
    energies = jnp.where(near == 1, energies[::-1], energies)
    rows = jnp.broadcast_to(virtual_energy[:, None], (virt_count, 128))
    energies, rows = lax.optimization_barrier((energies, rows))

    def partial(p):
        part = jnp.dot(own_t, kept[p], preferred_element_type=F32)
        part = part + jnp.dot(far_t, fetched[p], preferred_element_type=F32)
        part = part.astype(BF16)
        return part, lax.ppermute(part, "aux", within)

    def column(p):
        return energies[p // 2 : p // 2 + 1, (p % 2) * half : (p % 2 + 1) * half]

    def both(amp, rows_of):
        direct = 2.0 * jnp.dot(own, amp, preferred_element_type=F32)
        swapped = lax.dot_general(own[:, rows_of], amp, (((1,), (1,)), ((), ())), preferred_element_type=F32)
        return direct, swapped

    amps = [amplitude_piece(*partial(p), rows, column(p)) for p in range(3)]
    amp_shard = jnp.where(core == 1, amps[1], amps[0]).T
    direct, swapped = both(jnp.concatenate(amps[:2], axis=1), slice(None))
    near_density = (direct - swapped).astype(BF16)
    direct, swapped = both(amps[2], slice(0, half))
    part, other = partial(3)
    density = finish(near_arr, part, other, rows, column(3), own, direct, swapped, near_density)
    return (amp_shard, density)


def solution(mesh):
    n_aux, n_occ = mesh.shape["aux"], mesh.shape["occ"]
    fetch = n_aux == 2 * 2 and n_occ & (n_occ - 1) == 0
    return jax.shard_map(
        pair_shards if fetch else scatter_shards,
        mesh=mesh,
        in_specs=(P("aux", "occ", None), P("aux", "occ"), P("occ"), P(), P()),
        out_specs=(P(("occ", "aux"), None), P("aux", "occ", None)),
        check_vma=False,
    )
```

```python
import jax
import jax.numpy as jnp
from jax import lax
from jax.experimental import pallas as pl
from jax.experimental.pallas import tpu as pltpu
from jax.sharding import PartitionSpec as P

BF16 = jnp.bfloat16
F32 = jnp.float32


def lookup(entries, indices):
    positions = jnp.arange(entries.shape[0], dtype=jnp.int32)
    matches = indices[:, None] == positions[None, :]
    return jnp.sum(jnp.where(matches, entries[None, :], 0.0), axis=1)


def scatter_shards(factors, partner, occupied_energy, partner_energy, virtual_energy):
    aux_rows, local_occ, virt_count = factors.shape
    partner_full = lax.all_gather(partner, "occ", axis=1, tiled=True)
    flat_factors = factors.reshape(aux_rows, local_occ * virt_count)
    total_rows = local_occ * virt_count
    row_share = total_rows // lax.axis_size("aux")
    own_first = lax.axis_index("aux") * row_share
    integrals = lax.psum_scatter(
        lax.dot_general(flat_factors, partner_full, (((0,), (0,)), ((), ())), preferred_element_type=F32).astype(BF16),
        "aux",
        scatter_dimension=0,
        tiled=True,
    ).astype(F32)
    row_ids = own_first + jnp.arange(row_share, dtype=jnp.int32)
    occ_part = lookup(occupied_energy, row_ids // virt_count)
    virt_part = lookup(virtual_energy, row_ids % virt_count)
    divisor = virt_part[:, None] + virtual_energy[None, :] - occ_part[:, None] - partner_energy[0]
    amp_shard = (-integrals / divisor).astype(BF16)
    amp_full = lax.all_gather(amp_shard, "aux", axis=0, tiled=True)
    amp_cube = amp_full.reshape(local_occ, virt_count, virt_count)
    direct = jnp.einsum("qb,iab->qia", partner_full, amp_cube, preferred_element_type=F32)
    swapped = jnp.einsum("qb,iba->qia", partner_full, amp_cube, preferred_element_type=F32)
    density = (2.0 * direct - swapped).astype(BF16)
    return (amp_shard, density)


MIB = 1024 * 1024


def after(value, *others):
    return lax.optimization_barrier((value,) + others)[0]


def cost(flops, *arrays):
    moved = sum(a.size * a.dtype.itemsize for a in arrays)
    return pl.CostEstimate(flops=flops, bytes_accessed=moved, transcendentals=0)


def shaped(shape, dtype=BF16):
    return jax.ShapeDtypeStruct(shape, dtype)


def grant(mib):
    return pltpu.CompilerParams(vmem_limit_bytes=mib * MIB)


SCALAR = pl.BlockSpec(memory_space=pltpu.SMEM)
WHOLE = pl.BlockSpec(memory_space=pltpu.VMEM)


def turn(near_shard, far_shard):
    aux_rows, width = near_shard.shape

    def body(a_ref, b_ref, out_ref):
        out_ref[0] = a_ref[...].T
        out_ref[1] = b_ref[...].T

    return pl.pallas_call(
        body,
        in_specs=[WHOLE] * 2,
        out_specs=WHOLE,
        out_shape=shaped((2, width, aux_rows)),
        compiler_params=grant(8),
        cost_estimate=cost(0, near_shard, near_shard, far_shard, far_shard),
        name="turn_shards",
    )(near_shard, far_shard)


def assemble(here, blocks):
    _, width, aux_rows = blocks[0].shape
    virt_count = width * len(blocks)

    def body(here_ref, *refs):
        own_t_ref, far_t_ref, own_ref = refs[len(blocks) :]
        for k, ref in enumerate(refs[: len(blocks)]):
            first = pl.multiple_of((here_ref[0] ^ k) * width, width)
            own_t_ref[pl.ds(first, width), :] = ref[0]
            far_t_ref[pl.ds(first, width), :] = ref[1]
            own_ref[:, pl.ds(first, width)] = ref[0].T

    return pl.pallas_call(
        body,
        in_specs=[SCALAR] + [WHOLE] * len(blocks),
        out_specs=[WHOLE] * 3,
        out_shape=[shaped((virt_count, aux_rows))] * 2 + [shaped((aux_rows, virt_count))],
        compiler_params=grant(16),
        cost_estimate=cost(0, *blocks, *blocks),
        name="assemble_partner",
    )(here, *blocks)


def partial_integrals(own_t, far_t, kept, fetched):
    virt_count, aux_rows = own_t.shape
    share = kept.shape[1]
    block = virt_count // 4

    def body(own_ref, far_ref, kept_ref, fetched_ref, out_ref):
        total = jnp.dot(own_ref[...], kept_ref[...], preferred_element_type=F32)
        total += jnp.dot(far_ref[...], fetched_ref[...], preferred_element_type=F32)
        out_ref[...] = total.astype(BF16)

    band = pl.BlockSpec((block, aux_rows), lambda r: (r, 0))
    piece = pl.BlockSpec((aux_rows, share), lambda r: (0, 0))
    return pl.pallas_call(
        body,
        grid=(virt_count // block,),
        in_specs=[band, band, piece, piece],
        out_specs=pl.BlockSpec((block, share), lambda r: (r, 0)),
        out_shape=shaped((virt_count, share)),
        compiler_params=grant(16),
        cost_estimate=cost(4 * virt_count * aux_rows * share, own_t, far_t, kept, kept, own_t),
        name="partial_integrals",
    )(own_t, far_t, kept, fetched)


def amplitudes_of(part, other, row, column):
    wide = jnp.concatenate([row] * (part.shape[1] // row.shape[1]), axis=1)
    divisor = wide + column
    integrals = part.astype(F32) + other.astype(F32)
    inverse = pl.reciprocal(divisor, approx=True)
    inverse = inverse * (2.0 - divisor * inverse)
    return (-integrals * inverse).astype(BF16)


def amplitude_piece(part, other, rows, column):
    virt_count, share = part.shape
    block = virt_count // 4

    def body(part_ref, other_ref, row_ref, column_ref, out_ref):
        out_ref[...] = amplitudes_of(part_ref[...], other_ref[...], row_ref[...], column_ref[...])

    tile = pl.BlockSpec((block, share), lambda r: (r, 0))
    return pl.pallas_call(
        body,
        grid=(virt_count // block,),
        in_specs=[
            tile,
            tile,
            pl.BlockSpec((block, rows.shape[1]), lambda r: (r, 0)),
            pl.BlockSpec((1, share), lambda r: (0, 0)),
        ],
        out_specs=tile,
        out_shape=shaped(part.shape),
        compiler_params=grant(8),
        cost_estimate=cost(10 * part.size, part, part, part),
        name="amplitude_piece",
    )(part, other, rows, column)


def own_amplitudes(core, first, second):
    virt_count, share = first.shape
    block = virt_count // 4

    def body(core_ref, first_ref, second_ref, out_ref):
        out_ref[...] = jnp.where(core_ref[0] == 1, second_ref[...], first_ref[...]).T

    tile = pl.BlockSpec((block, share), lambda r: (r, 0))
    return pl.pallas_call(
        body,
        grid=(virt_count // block,),
        in_specs=[SCALAR, tile, tile],
        out_specs=pl.BlockSpec((share, block), lambda r: (0, r)),
        out_shape=shaped((share, virt_count)),
        compiler_params=grant(8),
        cost_estimate=cost(0, first, second, first),
        name="own_amplitudes",
    )(core, first, second)


def dot_rows(own, amp):
    return jnp.dot(own, amp, preferred_element_type=F32)


def dot_columns(own, amp):
    return lax.dot_general(own, amp, (((1,), (1,)), ((), ())), preferred_element_type=F32)


def density_terms(own, amps, dtype):
    aux_rows, virt_count = own.shape
    share = amps[0].shape[1]
    block = aux_rows // 4

    def body(own_ref, *refs):
        out_ref = refs[-1]
        rows = own_ref[...]
        twice = rows + rows
        swapped = jnp.zeros((block, virt_count), F32)
        for h, ref in enumerate(refs[:-1]):
            swapped += dot_columns(rows[:, h * share : (h + 1) * share], ref[...])
        for h in range(virt_count // share):
            at = slice(h * share, (h + 1) * share)
            if h < len(amps):
                out_ref[:, at] = (dot_rows(twice, refs[h][...]) - swapped[:, at]).astype(dtype)
            else:
                out_ref[:, at] = (-swapped[:, at]).astype(dtype)

    band = pl.BlockSpec((block, virt_count), lambda r: (r, 0))
    return pl.pallas_call(
        body,
        grid=(aux_rows // block,),
        in_specs=[band] + [pl.BlockSpec((virt_count, share), lambda r: (0, 0))] * len(amps),
        out_specs=band,
        out_shape=shaped((aux_rows, virt_count), dtype),
        compiler_params=grant(16),
        cost_estimate=cost(4 * aux_rows * virt_count * share * len(amps), own, own, *amps),
        name="density_terms",
    )(own, *amps)


def finish(near, part, other, rows, column, own, earlier, near_density):
    virt_count, share = part.shape
    aux_rows = own.shape[0]
    block = aux_rows // 4
    last = virt_count - share

    def body(near_ref, part_ref, other_ref, row_ref, column_ref, own_ref, earlier_ref, ready_ref, out_ref, amp_ref):
        @pl.when(pl.program_id(0) == 0)
        def _():
            amp_ref[...] = amplitudes_of(part_ref[...], other_ref[...], row_ref[...], column_ref[...])

        own_rows = own_ref[...]
        amp = amp_ref[...]
        swapped = dot_columns(own_rows[:, last:], amp)
        direct = dot_rows(own_rows + own_rows, amp)
        density = jnp.concatenate(
            [earlier_ref[:, :last] - swapped[:, :last], earlier_ref[:, last:] + (direct - swapped[:, last:])], axis=1
        ).astype(BF16)
        ready = ready_ref[...]
        swap = near_ref[0] == 1
        out_ref[:, 0, :] = jnp.where(swap, density, ready)
        out_ref[:, 1, :] = jnp.where(swap, ready, density)

    whole = lambda r: (0, 0)
    band = pl.BlockSpec((block, virt_count), lambda r: (r, 0))
    return pl.pallas_call(
        body,
        grid=(aux_rows // block,),
        in_specs=[
            SCALAR,
            pl.BlockSpec(part.shape, whole),
            pl.BlockSpec(other.shape, whole),
            pl.BlockSpec(rows.shape, whole),
            pl.BlockSpec((1, share), whole),
            band,
            band,
            band,
        ],
        out_specs=pl.BlockSpec((block, 2, virt_count), lambda r: (r, 0, 0)),
        out_shape=shaped((aux_rows, 2, virt_count)),
        scratch_shapes=[pltpu.VMEM(part.shape, BF16)],
        compiler_params=grant(24),
        cost_estimate=cost(4 * aux_rows * virt_count * share, part, other, own, earlier, near_density, near_density),
        name="finish_density",
    )(near, part, other, rows, column, own, earlier, near_density)


def pair_shards(factors, partner, occupied_energy, partner_energy, virtual_energy):
    aux_rows, local_occ, virt_count = factors.shape
    n_aux = lax.axis_size("aux")
    n_occ = lax.axis_size("occ")
    half = virt_count // 2
    across = [(d, (d + n_aux // 2) % n_aux) for d in range(n_aux)]
    within = [(d, d ^ 1) for d in range(n_aux)]
    place = lax.axis_index("aux")
    near, core = place // 2, place % 2
    as_scalar = lambda value: value.astype(jnp.int32).reshape(1)

    def occ_swap(value, k):
        return lax.ppermute(value, "occ", [(d, d ^ k) for d in range(n_occ)])

    flat = after(factors.reshape(aux_rows, local_occ * virt_count))
    halves = [flat[:, h * half : (h + 1) * half] for h in range(4)]
    kept = [jnp.where(near == 1, halves[h ^ 2], halves[h]) for h in range(4)]
    sent = kept[2:] + kept[:2]

    far = lax.ppermute(after(partner, sent[0]), "aux", across)
    fetched = [lax.ppermute(sent[0], "aux", across)]
    fetched.append(lax.ppermute(after(sent[1], far), "aux", across))
    for p in range(2, 4):
        fetched.append(lax.ppermute(after(sent[p], fetched[p - 2]), "aux", across))

    blocks = {0: turn(partner, far)}
    step = n_occ // 2
    while step > 1:
        for k in sorted(blocks):
            blocks[k + step] = occ_swap(blocks[k], step)
        step //= 2
    for k in sorted(blocks):
        blocks[k + 1] = occ_swap(blocks[k], 1)
    own_t, far_t, own = assemble(as_scalar(lax.axis_index("occ")), [blocks[k] for k in range(n_occ)])

    energies = virtual_energy[None, :] - occupied_energy[:, None] - partner_energy[0]
    energies = jnp.where(near == 1, energies[::-1], energies)
    rows = jnp.broadcast_to(virtual_energy[:, None], (virt_count, 128))
    energies, rows = lax.optimization_barrier((energies, rows))

    def exchanged(p):
        part = partial_integrals(own_t, far_t, kept[p], fetched[p])
        return part, lax.ppermute(part, "aux", within)

    def column(p):
        return energies[p // 2 : p // 2 + 1, (p % 2) * half : (p % 2 + 1) * half]

    amps = [amplitude_piece(*exchanged(p), rows, column(p)) for p in range(3)]
    near_density = density_terms(own, amps[:2], BF16)
    amp_shard = own_amplitudes(as_scalar(core), *amps[:2])
    earlier = density_terms(own, amps[2:], F32)
    part, other = exchanged(3)
    density = finish(as_scalar(near), part, other, rows, column(3), own, earlier, near_density)
    return (amp_shard, density)


def solution(mesh):
    n_aux, n_occ = mesh.shape["aux"], mesh.shape["occ"]
    fetch = n_aux == 2 * 2 and n_occ & (n_occ - 1) == 0
    return jax.shard_map(
        pair_shards if fetch else scatter_shards,
        mesh=mesh,
        in_specs=(P("aux", "occ", None), P("aux", "occ"), P("occ"), P(), P()),
        out_specs=(P(("occ", "aux"), None), P("aux", "occ", None)),
        check_vma=False,
    )
```

```python
import jax
import jax.numpy as jnp
from jax import lax
from jax.experimental import pallas as pl
from jax.experimental.pallas import tpu as pltpu
from jax.sharding import PartitionSpec as P

BF16 = jnp.bfloat16
F32 = jnp.float32


def lookup(entries, indices):
    positions = jnp.arange(entries.shape[0], dtype=jnp.int32)
    matches = indices[:, None] == positions[None, :]
    return jnp.sum(jnp.where(matches, entries[None, :], 0.0), axis=1)


def scatter_shards(factors, partner, occupied_energy, partner_energy, virtual_energy):
    aux_rows, local_occ, virt_count = factors.shape
    partner_full = lax.all_gather(partner, "occ", axis=1, tiled=True)
    flat_factors = factors.reshape(aux_rows, local_occ * virt_count)
    total_rows = local_occ * virt_count
    row_share = total_rows // lax.axis_size("aux")
    own_first = lax.axis_index("aux") * row_share
    integrals = lax.psum_scatter(
        lax.dot_general(flat_factors, partner_full, (((0,), (0,)), ((), ())), preferred_element_type=F32).astype(BF16),
        "aux",
        scatter_dimension=0,
        tiled=True,
    ).astype(F32)
    row_ids = own_first + jnp.arange(row_share, dtype=jnp.int32)
    occ_part = lookup(occupied_energy, row_ids // virt_count)
    virt_part = lookup(virtual_energy, row_ids % virt_count)
    divisor = virt_part[:, None] + virtual_energy[None, :] - occ_part[:, None] - partner_energy[0]
    amp_shard = (-integrals / divisor).astype(BF16)
    amp_full = lax.all_gather(amp_shard, "aux", axis=0, tiled=True)
    amp_cube = amp_full.reshape(local_occ, virt_count, virt_count)
    direct = jnp.einsum("qb,iab->qia", partner_full, amp_cube, preferred_element_type=F32)
    swapped = jnp.einsum("qb,iba->qia", partner_full, amp_cube, preferred_element_type=F32)
    density = (2.0 * direct - swapped).astype(BF16)
    return (amp_shard, density)


MIB = 1024 * 1024


def after(value, *others):
    return lax.optimization_barrier((value,) + others)[0]


def cost(flops, *arrays):
    moved = sum(a.size * a.dtype.itemsize for a in arrays)
    return pl.CostEstimate(flops=flops, bytes_accessed=moved, transcendentals=0)


def shaped(shape, dtype=BF16):
    return jax.ShapeDtypeStruct(shape, dtype)


def grant(mib):
    return pltpu.CompilerParams(vmem_limit_bytes=mib * MIB)


SCALAR = pl.BlockSpec(memory_space=pltpu.SMEM)
WHOLE = pl.BlockSpec(memory_space=pltpu.VMEM)


def turn(near_shard, far_shard, virtual_energy):
    aux_rows, width = near_shard.shape
    virt_count = virtual_energy.shape[1]
    lanes = 128

    def body(a_ref, b_ref, energy_ref, out_ref, rows_ref):
        out_ref[0] = a_ref[...].T
        out_ref[1] = b_ref[...].T
        rows_ref[...] = jnp.broadcast_to(energy_ref[...], (lanes, virt_count)).T

    return pl.pallas_call(
        body,
        in_specs=[WHOLE] * 3,
        out_specs=[WHOLE] * 2,
        out_shape=[shaped((2, width, aux_rows)), shaped((virt_count, lanes), F32)],
        compiler_params=grant(8),
        cost_estimate=cost(0, near_shard, near_shard, far_shard, far_shard),
        name="turn_shards",
    )(near_shard, far_shard, virtual_energy)


def assemble(here, blocks):
    _, width, aux_rows = blocks[0].shape
    virt_count = width * len(blocks)

    def body(here_ref, *refs):
        own_t_ref, far_t_ref, own_ref = refs[len(blocks) :]
        for k, ref in enumerate(refs[: len(blocks)]):
            first = pl.multiple_of((here_ref[0] ^ k) * width, width)
            own_t_ref[pl.ds(first, width), :] = ref[0]
            far_t_ref[pl.ds(first, width), :] = ref[1]
            own_ref[:, pl.ds(first, width)] = ref[0].T

    return pl.pallas_call(
        body,
        in_specs=[SCALAR] + [WHOLE] * len(blocks),
        out_specs=[WHOLE] * 3,
        out_shape=[shaped((virt_count, aux_rows))] * 2 + [shaped((aux_rows, virt_count))],
        compiler_params=grant(12),
        cost_estimate=cost(0, *blocks, *blocks),
        name="assemble_partner",
    )(here, *blocks)


def partial_integrals(own_t, far_t, kept, fetched):
    virt_count, aux_rows = own_t.shape
    share = kept.shape[1]
    block = virt_count // 4

    def body(own_ref, far_ref, kept_ref, fetched_ref, out_ref):
        @pl.loop(0, virt_count // block)
        def _(r):
            band = pl.ds(pl.multiple_of(r * block, block), block)
            total = jnp.dot(own_ref[band, :], kept_ref[...], preferred_element_type=F32)
            total += jnp.dot(far_ref[band, :], fetched_ref[...], preferred_element_type=F32)
            out_ref[band, :] = total.astype(BF16)

    return pl.pallas_call(
        body,
        in_specs=[WHOLE] * 4,
        out_specs=WHOLE,
        out_shape=shaped((virt_count, share)),
        compiler_params=grant(12),
        cost_estimate=cost(4 * virt_count * aux_rows * share, own_t, far_t, kept, kept, own_t),
        name="partial_integrals",
    )(own_t, far_t, kept, fetched)


def amplitude_bands(energy_refs, occupied, first, part_ref, other_ref, out_ref):
    place_ref, occupied_ref, partner_ref, virtual_ref, rows_ref = energy_refs
    virt_count, share = part_ref.shape
    lanes = rows_ref.shape[1]
    block = virt_count // 8
    resident = occupied_ref[jnp.where(place_ref[0] == 1, 1 - occupied, occupied)]
    column = virtual_ref[:, first : first + share] - resident - partner_ref[0]

    @pl.loop(0, virt_count // block)
    def _(r):
        band = pl.ds(pl.multiple_of(r * block, block), block)
        divisor = jnp.concatenate([rows_ref[band, :]] * (share // lanes), axis=1) + column
        integrals = part_ref[band, :].astype(F32) + other_ref[band, :].astype(F32)
        inverse = pl.reciprocal(divisor, approx=True)
        inverse = inverse * (2.0 - divisor * inverse)
        out_ref[band, :] = (-integrals * inverse).astype(BF16)


ENERGY_SPECS = [SCALAR, SCALAR, SCALAR, WHOLE, WHOLE]


def amplitude_piece(energies, occupied, first, part, other):
    def body(*refs):
        amplitude_bands(refs[:5], occupied, first, *refs[5:])

    return pl.pallas_call(
        body,
        in_specs=ENERGY_SPECS + [WHOLE] * 2,
        out_specs=WHOLE,
        out_shape=shaped(part.shape),
        compiler_params=grant(12),
        cost_estimate=cost(10 * part.size, part, part, part),
        name="amplitude_piece",
    )(*energies, part, other)


def own_amplitudes(core, first, second):
    virt_count, share = first.shape
    block = virt_count // 4

    def body(core_ref, first_ref, second_ref, out_ref):
        for r in range(virt_count // block):
            band = slice(r * block, (r + 1) * block)
            out_ref[:, band] = jnp.where(core_ref[0] == 1, second_ref[band, :], first_ref[band, :]).T

    return pl.pallas_call(
        body,
        in_specs=[SCALAR, WHOLE, WHOLE],
        out_specs=WHOLE,
        out_shape=shaped((share, virt_count)),
        compiler_params=grant(12),
        cost_estimate=cost(0, first, second, first),
        name="own_amplitudes",
    )(core, first, second)


def dot_rows(own, amp):
    return jnp.dot(own, amp, preferred_element_type=F32)


def dot_columns(own, amp):
    return lax.dot_general(own, amp, (((1,), (1,)), ((), ())), preferred_element_type=F32)


def density_terms(own, amps, dtype):
    aux_rows, virt_count = own.shape
    share = amps[0].shape[1]
    block = share // 2

    def body(own_ref, *refs):
        out_ref = refs[-1]
        for n in range(virt_count // block):
            at = slice(n * block, (n + 1) * block)
            total = jnp.zeros((aux_rows, block), F32)
            for h, ref in enumerate(refs[:-1]):
                total -= dot_columns(own_ref[:, h * share : (h + 1) * share], ref[at, :])
            h, first = n * block // share, n * block % share
            if h < len(amps):
                rows = own_ref[...]
                total += dot_rows(rows + rows, refs[h][:, first : first + block])
            out_ref[:, at] = total.astype(dtype)

    return pl.pallas_call(
        body,
        in_specs=[WHOLE] * (1 + len(amps)),
        out_specs=WHOLE,
        out_shape=shaped((aux_rows, virt_count), dtype),
        compiler_params=grant(16),
        cost_estimate=cost(4 * aux_rows * virt_count * share * len(amps), own, own, *amps),
        name="density_terms",
    )(own, *amps)


def finish(energies, first, part, other, own, earlier, near_density):
    virt_count, share = part.shape
    aux_rows = own.shape[0]
    block = share // 2

    def body(*refs):
        energy_refs, (part_ref, other_ref, own_ref, earlier_ref, ready_ref, out_ref, amp_ref) = refs[:5], refs[5:]
        step = pl.program_id(0)

        @pl.when(step == 0)
        def _():
            amplitude_bands(energy_refs, 1, first, part_ref, other_ref, amp_ref)

        swap = energy_refs[0][0] == 1
        for n in range(virt_count // block):

            @pl.when(step == n)
            def _():
                at = slice(n * block, (n + 1) * block)
                total = earlier_ref[:, at] - dot_columns(own_ref[:, first:], amp_ref[at, :])
                if n * block >= first:
                    rows = own_ref[...]
                    total += dot_rows(rows + rows, amp_ref[:, n * block - first : (n + 1) * block - first])
                density = total.astype(BF16)
                ready = ready_ref[:, at]
                out_ref[:, 0, :] = jnp.where(swap, density, ready)
                out_ref[:, 1, :] = jnp.where(swap, ready, density)

    return pl.pallas_call(
        body,
        grid=(virt_count // block,),
        in_specs=ENERGY_SPECS + [WHOLE] * 5,
        out_specs=pl.BlockSpec((aux_rows, 2, block), lambda n: (0, 0, n)),
        out_shape=shaped((aux_rows, 2, virt_count)),
        scratch_shapes=[pltpu.VMEM(part.shape, BF16)],
        compiler_params=grant(20),
        cost_estimate=cost(4 * aux_rows * virt_count * share, part, other, own, earlier, near_density, near_density),
        name="finish_density",
    )(*energies, part, other, own, earlier, near_density)


def pair_shards(factors, partner, occupied_energy, partner_energy, virtual_energy):
    aux_rows, local_occ, virt_count = factors.shape
    n_aux = lax.axis_size("aux")
    n_occ = lax.axis_size("occ")
    half = virt_count // 2
    across = [(d, (d + n_aux // 2) % n_aux) for d in range(n_aux)]
    within = [(d, d ^ 1) for d in range(n_aux)]
    place = lax.axis_index("aux")
    near, core = place // 2, place % 2
    as_scalar = lambda value: value.astype(jnp.int32).reshape(1)

    def occ_swap(value, k):
        return lax.ppermute(value, "occ", [(d, d ^ k) for d in range(n_occ)])

    far = lax.ppermute(partner, "aux", across)

    flat = after(factors.reshape(aux_rows, local_occ * virt_count))
    halves = [flat[:, h * half : (h + 1) * half] for h in range(4)]
    kept = [jnp.where(near == 1, halves[h ^ 2], halves[h]) for h in range(4)]
    sent = kept[2:] + kept[:2]
    fetched = [lax.ppermute(piece, "aux", across) for piece in sent[:2]]
    fetched.append(lax.ppermute(after(sent[2], fetched[0]), "aux", across))
    fetched.append(lax.ppermute(after(sent[3], fetched[2]), "aux", across))

    line = virtual_energy.reshape(1, virt_count)
    shard, rows = turn(partner, far, line)
    energies = (as_scalar(near), occupied_energy, partner_energy, line, rows)

    blocks = {0: shard}
    step = n_occ // 2
    while step > 1:
        for k in sorted(blocks):
            blocks[k + step] = occ_swap(blocks[k], step)
        step //= 2
    previous = None
    for k in sorted(blocks, key=lambda k: (bin(k).count("1"), k)):
        blocks[k + 1] = occ_swap(blocks[k] if previous is None else after(blocks[k], previous), 1)
        previous = blocks[k + 1]
    own_t, far_t, own = assemble(as_scalar(lax.axis_index("occ")), [blocks[k] for k in range(n_occ)])

    def exchanged(p, *earlier):
        part = partial_integrals(own_t, far_t, after(kept[p], *earlier), fetched[p])
        return part, lax.ppermute(part, "aux", within)

    first, second = exchanged(0), exchanged(1)
    amps = [amplitude_piece(energies, 0, 0, *first), amplitude_piece(energies, 0, half, *second)]
    near_density = density_terms(own, amps, BF16)
    amp_shard = own_amplitudes(as_scalar(core), *amps)
    amp = amplitude_piece(energies, 1, 0, *exchanged(2, near_density, amp_shard))
    earlier = density_terms(own, [amp], F32)
    density = finish(energies, half, *exchanged(3, earlier), own, earlier, near_density)
    return (amp_shard, density)


MIB = 1024 * 1024


def after(value, *others):
    return lax.optimization_barrier((value,) + others)[0]


def cost(flops, *arrays):
    moved = sum(a.size * a.dtype.itemsize for a in arrays)
    return pl.CostEstimate(flops=flops, bytes_accessed=moved, transcendentals=0)


def shaped(shape, dtype=BF16):
    return jax.ShapeDtypeStruct(shape, dtype)


def grant(mib):
    return pltpu.CompilerParams(vmem_limit_bytes=mib * MIB)


SCALAR = pl.BlockSpec(memory_space=pltpu.SMEM)
WHOLE = pl.BlockSpec(memory_space=pltpu.VMEM)


def turn(near_shard, far_shard, virtual_energy):
    aux_rows, width = near_shard.shape
    virt_count = virtual_energy.shape[1]
    lanes = 128

    def body(a_ref, b_ref, energy_ref, out_ref, rows_ref):
        out_ref[0] = a_ref[...].T
        out_ref[1] = b_ref[...].T
        rows_ref[...] = jnp.broadcast_to(energy_ref[...], (lanes, virt_count)).T

    return pl.pallas_call(
        body,
        in_specs=[WHOLE] * 3,
        out_specs=[WHOLE] * 2,
        out_shape=[shaped((2, width, aux_rows)), shaped((virt_count, lanes), F32)],
        compiler_params=grant(8),
        cost_estimate=cost(0, near_shard, near_shard, far_shard, far_shard),
        name="turn_shards",
    )(near_shard, far_shard, virtual_energy)


def assemble(here, blocks):
    _, width, aux_rows = blocks[0].shape
    virt_count = width * len(blocks)

    def body(here_ref, *refs):
        own_t_ref, far_t_ref, own_ref = refs[len(blocks) :]
        for k, ref in enumerate(refs[: len(blocks)]):
            first = pl.multiple_of((here_ref[0] ^ k) * width, width)
            own_t_ref[pl.ds(first, width), :] = ref[0]
            far_t_ref[pl.ds(first, width), :] = ref[1]
            own_ref[:, pl.ds(first, width)] = ref[0].T

    return pl.pallas_call(
        body,
        in_specs=[SCALAR] + [WHOLE] * len(blocks),
        out_specs=[WHOLE] * 3,
        out_shape=[shaped((virt_count, aux_rows))] * 2 + [shaped((aux_rows, virt_count))],
        compiler_params=grant(12),
        cost_estimate=cost(0, *blocks, *blocks),
        name="assemble_partner",
    )(here, *blocks)


def partial_integrals(own_t, far_t, kept, fetched):
    virt_count, aux_rows = own_t.shape
    share = kept.shape[1]
    block = virt_count // 4

    def body(own_ref, far_ref, kept_ref, fetched_ref, out_ref):
        @pl.loop(0, virt_count // block)
        def _(r):
            band = pl.ds(pl.multiple_of(r * block, block), block)
            total = jnp.dot(own_ref[band, :], kept_ref[...], preferred_element_type=F32)
            total += jnp.dot(far_ref[band, :], fetched_ref[...], preferred_element_type=F32)
            out_ref[band, :] = total.astype(BF16)

    return pl.pallas_call(
        body,
        in_specs=[WHOLE] * 4,
        out_specs=WHOLE,
        out_shape=shaped((virt_count, share)),
        compiler_params=grant(12),
        cost_estimate=cost(4 * virt_count * aux_rows * share, own_t, far_t, kept, kept, own_t),
        name="partial_integrals",
    )(own_t, far_t, kept, fetched)


def amplitude_bands(energy_refs, occupied, first, part_ref, other_ref, out_ref):
    place_ref, occupied_ref, partner_ref, virtual_ref, rows_ref = energy_refs
    virt_count, share = part_ref.shape
    lanes = rows_ref.shape[1]
    block = virt_count // 8
    resident = occupied_ref[jnp.where(place_ref[0] == 1, 1 - occupied, occupied)]
    column = virtual_ref[:, first : first + share] - resident - partner_ref[0]

    @pl.loop(0, virt_count // block)
    def _(r):
        band = pl.ds(pl.multiple_of(r * block, block), block)
        divisor = jnp.concatenate([rows_ref[band, :]] * (share // lanes), axis=1) + column
        integrals = part_ref[band, :].astype(F32) + other_ref[band, :].astype(F32)
        inverse = pl.reciprocal(divisor, approx=True)
        inverse = inverse * (2.0 - divisor * inverse)
        out_ref[band, :] = (-integrals * inverse).astype(BF16)


ENERGY_SPECS = [SCALAR, SCALAR, SCALAR, WHOLE, WHOLE]


def amplitude_piece(energies, occupied, first, part, other):
    def body(*refs):
        amplitude_bands(refs[:5], occupied, first, *refs[5:])

    return pl.pallas_call(
        body,
        in_specs=ENERGY_SPECS + [WHOLE] * 2,
        out_specs=WHOLE,
        out_shape=shaped(part.shape),
        compiler_params=grant(12),
        cost_estimate=cost(10 * part.size, part, part, part),
        name="amplitude_piece",
    )(*energies, part, other)


def own_amplitudes(core, first, second):
    virt_count, share = first.shape
    block = virt_count // 4

    def body(core_ref, first_ref, second_ref, out_ref):
        for r in range(virt_count // block):
            band = slice(r * block, (r + 1) * block)
            out_ref[:, band] = jnp.where(core_ref[0] == 1, second_ref[band, :], first_ref[band, :]).T

    return pl.pallas_call(
        body,
        in_specs=[SCALAR, WHOLE, WHOLE],
        out_specs=WHOLE,
        out_shape=shaped((share, virt_count)),
        compiler_params=grant(12),
        cost_estimate=cost(0, first, second, first),
        name="own_amplitudes",
    )(core, first, second)


def dot_rows(own, amp):
    return jnp.dot(own, amp, preferred_element_type=F32)


def dot_columns(own, amp):
    return lax.dot_general(own, amp, (((1,), (1,)), ((), ())), preferred_element_type=F32)


def density_terms(own, amps, dtype):
    aux_rows, virt_count = own.shape
    share = amps[0].shape[1]
    block = share // 2

    def body(own_ref, *refs):
        out_ref = refs[-1]
        for n in range(virt_count // block):
            at = slice(n * block, (n + 1) * block)
            total = jnp.zeros((aux_rows, block), F32)
            for h, ref in enumerate(refs[:-1]):
                total -= dot_columns(own_ref[:, h * share : (h + 1) * share], ref[at, :])
            h, first = n * block // share, n * block % share
            if h < len(amps):
                rows = own_ref[...]
                total += dot_rows(rows + rows, refs[h][:, first : first + block])
            out_ref[:, at] = total.astype(dtype)

    return pl.pallas_call(
        body,
        in_specs=[WHOLE] * (1 + len(amps)),
        out_specs=WHOLE,
        out_shape=shaped((aux_rows, virt_count), dtype),
        compiler_params=grant(16),
        cost_estimate=cost(4 * aux_rows * virt_count * share * len(amps), own, own, *amps),
        name="density_terms",
    )(own, *amps)


def finish(energies, first, part, other, own, earlier, near_density):
    virt_count, share = part.shape
    aux_rows = own.shape[0]
    block = share // 2

    def body(*refs):
        energy_refs, (part_ref, other_ref, own_ref, earlier_ref, ready_ref, out_ref, amp_ref) = refs[:5], refs[5:]
        step = pl.program_id(0)

        @pl.when(step == 0)
        def _():
            amplitude_bands(energy_refs, 1, first, part_ref, other_ref, amp_ref)

        swap = energy_refs[0][0] == 1
        for n in range(virt_count // block):

            @pl.when(step == n)
            def _():
                at = slice(n * block, (n + 1) * block)
                total = earlier_ref[:, at] - dot_columns(own_ref[:, first:], amp_ref[at, :])
                if n * block >= first:
                    rows = own_ref[...]
                    total += dot_rows(rows + rows, amp_ref[:, n * block - first : (n + 1) * block - first])
                density = total.astype(BF16)
                ready = ready_ref[:, at]
                out_ref[:, 0, :] = jnp.where(swap, density, ready)
                out_ref[:, 1, :] = jnp.where(swap, ready, density)

    return pl.pallas_call(
        body,
        grid=(virt_count // block,),
        in_specs=ENERGY_SPECS + [WHOLE] * 5,
        out_specs=pl.BlockSpec((aux_rows, 2, block), lambda n: (0, 0, n)),
        out_shape=shaped((aux_rows, 2, virt_count)),
        scratch_shapes=[pltpu.VMEM(part.shape, BF16)],
        compiler_params=grant(20),
        cost_estimate=cost(4 * aux_rows * virt_count * share, part, other, own, earlier, near_density, near_density),
        name="finish_density",
    )(*energies, part, other, own, earlier, near_density)


def pair_shards(factors, partner, occupied_energy, partner_energy, virtual_energy):
    aux_rows, local_occ, virt_count = factors.shape
    n_aux = lax.axis_size("aux")
    n_occ = lax.axis_size("occ")
    half = virt_count // 2
    across = [(d, (d + n_aux // 2) % n_aux) for d in range(n_aux)]
    within = [(d, d ^ 1) for d in range(n_aux)]
    place = lax.axis_index("aux")
    near, core = place // 2, place % 2
    as_scalar = lambda value: value.astype(jnp.int32).reshape(1)

    def occ_swap(value, k):
        return lax.ppermute(value, "occ", [(d, d ^ k) for d in range(n_occ)])

    far = lax.ppermute(partner, "aux", across)

    flat = after(factors.reshape(aux_rows, local_occ * virt_count))
    halves = [flat[:, h * half : (h + 1) * half] for h in range(4)]
    kept = [jnp.where(near == 1, halves[h ^ 2], halves[h]) for h in range(4)]
    sent = kept[2:] + kept[:2]
    fetched = [lax.ppermute(piece, "aux", across) for piece in sent[:2]]
    fetched.append(lax.ppermute(after(sent[2], fetched[0]), "aux", across))
    fetched.append(lax.ppermute(after(sent[3], fetched[2]), "aux", across))

    line = virtual_energy.reshape(1, virt_count)
    shard, rows = turn(partner, far, line)
    energies = (as_scalar(near), occupied_energy, partner_energy, line, rows)

    blocks = {0: shard}
    step = n_occ // 2
    while step > 1:
        for k in sorted(blocks):
            blocks[k + step] = occ_swap(blocks[k], step)
        step //= 2
    previous = None
    for k in sorted(blocks, key=lambda k: (bin(k).count("1"), k)):
        blocks[k + 1] = occ_swap(blocks[k] if previous is None else after(blocks[k], previous), 1)
        previous = blocks[k + 1]
    own_t, far_t, own = assemble(as_scalar(lax.axis_index("occ")), [blocks[k] for k in range(n_occ)])

    def exchanged(p):
        part = partial_integrals(own_t, far_t, kept[p], fetched[p])
        return part, lax.ppermute(part, "aux", within)

    def at(p):
        return p // 2, p % 2 * half

    amps = [amplitude_piece(energies, *at(p), *exchanged(p)) for p in range(3)]
    near_density = density_terms(own, amps[:2], BF16)
    amp_shard = own_amplitudes(as_scalar(core), *amps[:2])
    earlier = density_terms(own, amps[2:], F32)
    density = finish(energies, half, *exchanged(3), own, earlier, near_density)
    return (amp_shard, density)


def solution(mesh):
    n_aux, n_occ = mesh.shape["aux"], mesh.shape["occ"]
    fetch = n_aux == 2 * 2 and n_occ & (n_occ - 1) == 0
    return jax.shard_map(
        pair_shards if fetch else scatter_shards,
        mesh=mesh,
        in_specs=(P("aux", "occ", None), P("aux", "occ"), P("occ"), P(), P()),
        out_specs=(P(("occ", "aux"), None), P("aux", "occ", None)),
        check_vma=False,
    )
```

```python
import jax
import jax.numpy as jnp
from jax import lax
from jax.experimental import pallas as pl
from jax.experimental.pallas import tpu as pltpu
from jax.sharding import PartitionSpec as P

BF16 = jnp.bfloat16
F32 = jnp.float32


def lookup(entries, indices):
    positions = jnp.arange(entries.shape[0], dtype=jnp.int32)
    matches = indices[:, None] == positions[None, :]
    return jnp.sum(jnp.where(matches, entries[None, :], 0.0), axis=1)


def scatter_shards(factors, partner, occupied_energy, partner_energy, virtual_energy):
    aux_rows, local_occ, virt_count = factors.shape
    partner_full = lax.all_gather(partner, "occ", axis=1, tiled=True)
    flat_factors = factors.reshape(aux_rows, local_occ * virt_count)
    total_rows = local_occ * virt_count
    row_share = total_rows // lax.axis_size("aux")
    own_first = lax.axis_index("aux") * row_share
    integrals = lax.psum_scatter(
        lax.dot_general(flat_factors, partner_full, (((0,), (0,)), ((), ())), preferred_element_type=F32).astype(BF16),
        "aux",
        scatter_dimension=0,
        tiled=True,
    ).astype(F32)
    row_ids = own_first + jnp.arange(row_share, dtype=jnp.int32)
    occ_part = lookup(occupied_energy, row_ids // virt_count)
    virt_part = lookup(virtual_energy, row_ids % virt_count)
    divisor = virt_part[:, None] + virtual_energy[None, :] - occ_part[:, None] - partner_energy[0]
    amp_shard = (-integrals / divisor).astype(BF16)
    amp_full = lax.all_gather(amp_shard, "aux", axis=0, tiled=True)
    amp_cube = amp_full.reshape(local_occ, virt_count, virt_count)
    direct = jnp.einsum("qb,iab->qia", partner_full, amp_cube, preferred_element_type=F32)
    swapped = jnp.einsum("qb,iba->qia", partner_full, amp_cube, preferred_element_type=F32)
    density = (2.0 * direct - swapped).astype(BF16)
    return (amp_shard, density)


MIB = 1024 * 1024


def cost(flops, *arrays):
    return pl.CostEstimate(flops=1, bytes_accessed=1, transcendentals=0)


def shaped(shape, dtype=BF16):
    return jax.ShapeDtypeStruct(shape, dtype)


def grant(mib):
    return pltpu.CompilerParams(vmem_limit_bytes=mib * MIB)


SCALAR = pl.BlockSpec(memory_space=pltpu.SMEM)
WHOLE = pl.BlockSpec(memory_space=pltpu.VMEM)
UNREAD = pl.BlockSpec(memory_space=pl.ANY)
LANES = 128


def turn(places, near_shard, far_shard, occupied_energy, partner_energy, virtual_energy):
    aux_rows, width = near_shard.shape
    virt_count = virtual_energy.shape[1]

    def body(places_ref, a_ref, b_ref, occupied_ref, partner_ref, energy_ref, out_ref, rows_ref, columns_ref):
        out_ref[0] = a_ref[...].T
        out_ref[1] = b_ref[...].T
        rows_ref[...] = jnp.broadcast_to(energy_ref[...], (LANES, virt_count)).T
        near = places_ref[0]
        for i in range(2):
            resident = occupied_ref[jnp.where(near == 1, 1 - i, i)]
            columns_ref[i : i + 1, :] = energy_ref[...] - resident - partner_ref[0]

    return pl.pallas_call(
        body,
        in_specs=[SCALAR, WHOLE, WHOLE, SCALAR, SCALAR, WHOLE],
        out_specs=[WHOLE] * 3,
        out_shape=[shaped((2, width, aux_rows)), shaped((virt_count, LANES), F32), shaped((2, virt_count), F32)],
        compiler_params=grant(8),
        cost_estimate=cost(0, near_shard, near_shard, far_shard, far_shard),
        name="turn_shards",
    )(places, near_shard, far_shard, occupied_energy, partner_energy, virtual_energy)


def pick(places, flat, p, *earlier):
    aux_rows, width = flat.shape
    half = width // 4

    def body(places_ref, flat_ref, *refs):
        h = jnp.where(places_ref[0] == 1, p ^ 2, p)
        refs[-1][...] = flat_ref[:, pl.ds(pl.multiple_of(h * half, half), half)]

    return pl.pallas_call(
        body,
        in_specs=[SCALAR, WHOLE] + [UNREAD] * len(earlier),
        out_specs=WHOLE,
        out_shape=shaped((aux_rows, half)),
        compiler_params=grant(8),
        cost_estimate=cost(0, flat),
        name="pick_piece",
    )(places, flat, *earlier)


def assemble(places, blocks):
    _, width, aux_rows = blocks[0].shape
    virt_count = width * len(blocks)

    def body(places_ref, *refs):
        own_t_ref, far_t_ref, own_ref = refs[len(blocks) :]
        for k, ref in enumerate(refs[: len(blocks)]):
            first = pl.multiple_of((places_ref[2] ^ k) * width, width)
            own_t_ref[pl.ds(first, width), :] = ref[0]
            far_t_ref[pl.ds(first, width), :] = ref[1]
            own_ref[:, pl.ds(first, width)] = ref[0].T

    return pl.pallas_call(
        body,
        in_specs=[SCALAR] + [WHOLE] * len(blocks),
        out_specs=[WHOLE] * 3,
        out_shape=[shaped((virt_count, aux_rows))] * 2 + [shaped((aux_rows, virt_count))],
        compiler_params=grant(12),
        cost_estimate=cost(0, *blocks, *blocks),
        name="assemble_partner",
    )(places, *blocks)


def partial_integrals(own_t, far_t, kept, fetched, *earlier):
    virt_count, aux_rows = own_t.shape
    share = kept.shape[1]
    block = share // 2

    def body(own_ref, far_ref, kept_ref, fetched_ref, *refs):
        for n in range(share // block):
            at = slice(n * block, (n + 1) * block)
            total = dot_rows(own_ref[...], kept_ref[:, at])
            total += dot_rows(far_ref[...], fetched_ref[:, at])
            refs[-1][:, at] = total.astype(BF16)

    return pl.pallas_call(
        body,
        in_specs=[WHOLE] * 4 + [UNREAD] * len(earlier),
        out_specs=WHOLE,
        out_shape=shaped((virt_count, share)),
        compiler_params=grant(12),
        cost_estimate=cost(4 * virt_count * aux_rows * share, own_t, far_t, kept, kept, own_t),
        name="partial_integrals",
    )(own_t, far_t, kept, fetched, *earlier)


def amplitude_bands(rows_ref, columns_ref, i, first, part_ref, other_ref, out_ref):
    virt_count, share = part_ref.shape
    block = 32
    column = jnp.broadcast_to(columns_ref[i : i + 1, first : first + share], (8, share))

    @pl.loop(0, virt_count // block, unroll=2)
    def _(r):
        band = pl.ds(pl.multiple_of(r * block, block), block)
        divisor = jnp.concatenate([rows_ref[band, :]] * (share // LANES), axis=1)
        divisor = divisor + jnp.concatenate([column] * (block // 8), axis=0)
        integrals = part_ref[band, :].astype(F32) + other_ref[band, :].astype(F32)
        inverse = pl.reciprocal(divisor, approx=True)
        inverse = inverse * (divisor * inverse - 2.0)
        out_ref[band, :] = (integrals * inverse).astype(BF16)


def amplitude_piece(rows, columns, i, first, part, other):
    def body(rows_ref, columns_ref, part_ref, other_ref, out_ref):
        amplitude_bands(rows_ref, columns_ref, i, first, part_ref, other_ref, out_ref)

    return pl.pallas_call(
        body,
        in_specs=[WHOLE] * 4,
        out_specs=WHOLE,
        out_shape=shaped(part.shape),
        compiler_params=grant(12),
        cost_estimate=cost(10 * part.size, part, part, part),
        name="amplitude_piece",
    )(rows, columns, part, other)


def own_amplitudes(places, first, second):
    virt_count, share = first.shape
    block = virt_count // 4

    def body(places_ref, first_ref, second_ref, out_ref):
        for r in range(virt_count // block):
            band = slice(r * block, (r + 1) * block)
            out_ref[:, band] = jnp.where(places_ref[1] == 1, second_ref[band, :], first_ref[band, :]).T

    return pl.pallas_call(
        body,
        in_specs=[SCALAR, WHOLE, WHOLE],
        out_specs=WHOLE,
        out_shape=shaped((share, virt_count)),
        compiler_params=grant(12),
        cost_estimate=cost(0, first, second, first),
        name="own_amplitudes",
    )(places, first, second)


def dot_rows(own, amp):
    return jnp.dot(own, amp, preferred_element_type=F32)


def dot_columns(own, amp):
    return lax.dot_general(own, amp, (((1,), (1,)), ((), ())), preferred_element_type=F32)


def density_terms(own, amps, dtype):
    aux_rows, virt_count = own.shape
    share = amps[0].shape[1]
    block = share // 2

    def body(own_ref, *refs):
        out_ref = refs[-1]
        for n in range(virt_count // block):
            at = slice(n * block, (n + 1) * block)
            total = jnp.zeros((aux_rows, block), F32)
            for h, ref in enumerate(refs[:-1]):
                total -= dot_columns(own_ref[:, h * share : (h + 1) * share], ref[at, :])
            h, first = n * block // share, n * block % share
            if h < len(amps):
                rows = own_ref[...]
                total += dot_rows(rows + rows, refs[h][:, first : first + block])
            out_ref[:, at] = total.astype(dtype)

    return pl.pallas_call(
        body,
        in_specs=[WHOLE] * (1 + len(amps)),
        out_specs=WHOLE,
        out_shape=shaped((aux_rows, virt_count), dtype),
        compiler_params=grant(16),
        cost_estimate=cost(4 * aux_rows * virt_count * share * len(amps), own, own, *amps),
        name="density_terms",
    )(own, *amps)


def finish(places, rows, columns, first, part, other, own, earlier, near_density):
    virt_count, share = part.shape
    aux_rows = own.shape[0]
    block = share // 2

    def body(*refs):
        places_ref, rows_ref, columns_ref, part_ref, other_ref, own_ref, earlier_ref, ready_ref, out_ref, amp_ref = refs
        step = pl.program_id(0)

        @pl.when(step == 0)
        def _():
            amplitude_bands(rows_ref, columns_ref, 1, first, part_ref, other_ref, amp_ref)

        swap = places_ref[0] == 1
        for n in range(virt_count // block):

            @pl.when(step == n)
            def _():
                at = slice(n * block, (n + 1) * block)
                total = earlier_ref[:, at] - dot_columns(own_ref[:, first:], amp_ref[at, :])
                if n * block >= first:
                    rows = own_ref[...]
                    total += dot_rows(rows + rows, amp_ref[:, n * block - first : (n + 1) * block - first])
                density = total.astype(BF16)
                ready = ready_ref[:, at]
                out_ref[:, 0, :] = jnp.where(swap, density, ready)
                out_ref[:, 1, :] = jnp.where(swap, ready, density)

    return pl.pallas_call(
        body,
        grid=(virt_count // block,),
        in_specs=[SCALAR] + [WHOLE] * 7,
        out_specs=pl.BlockSpec((aux_rows, 2, block), lambda n: (0, 0, n)),
        out_shape=shaped((aux_rows, 2, virt_count)),
        scratch_shapes=[pltpu.VMEM(part.shape, BF16)],
        compiler_params=grant(20),
        cost_estimate=cost(4 * aux_rows * virt_count * share, part, other, own, earlier, near_density, near_density),
        name="finish_density",
    )(places, rows, columns, part, other, own, earlier, near_density)


def pair_shards(factors, partner, occupied_energy, partner_energy, virtual_energy):
    aux_rows, local_occ, virt_count = factors.shape
    n_aux = lax.axis_size("aux")
    n_occ = lax.axis_size("occ")
    half = virt_count // 2
    across = [(d, (d + n_aux // 2) % n_aux) for d in range(n_aux)]
    within = [(d, d ^ 1) for d in range(n_aux)]
    place = lax.axis_index("aux")
    places = jnp.stack([place // 2, place % 2, lax.axis_index("occ")]).astype(jnp.int32)
    places, partner, factors = lax.optimization_barrier((places, partner, factors))

    def occ_swap(value, k):
        return lax.ppermute(value, "occ", [(d, d ^ k) for d in range(n_occ)])

    far = lax.ppermute(partner, "aux", across)

    flat = factors.reshape(aux_rows, local_occ * virt_count)
    kept, fetched = [None] * 4, []
    for p in range(4):
        h = p ^ 2
        kept[h] = pick(places, flat, h, *(fetched if p > 1 else []))
        fetched.append(lax.ppermute(kept[h], "aux", across))

    shard, rows, columns = turn(places, partner, far, occupied_energy, partner_energy, virtual_energy.reshape(1, virt_count))
    blocks = {0: shard}
    step = n_occ // 2
    while step > 1:
        for k in sorted(blocks):
            blocks[k + step] = occ_swap(blocks[k], step)
        step //= 2
    for k in sorted(blocks):
        blocks[k + 1] = occ_swap(blocks[k], 1)
    own_t, far_t, own = assemble(places, [blocks[k] for k in range(n_occ)])

    def exchanged(p, *earlier):
        part = partial_integrals(own_t, far_t, kept[p], fetched[p], *earlier)
        return part, lax.ppermute(part, "aux", within)

    first = exchanged(0)
    second = exchanged(1, first[0])
    amps = [amplitude_piece(rows, columns, 0, 0, *first), amplitude_piece(rows, columns, 0, half, *second)]
    near_density = density_terms(own, amps, BF16)
    amp_shard = own_amplitudes(places, *amps)
    third = exchanged(2, near_density)
    amp = amplitude_piece(rows, columns, 1, 0, *third)
    earlier = density_terms(own, [amp], F32)
    last = exchanged(3, earlier, amp_shard)
    density = finish(places, rows, columns, half, *last, own, earlier, near_density)
    return (amp_shard, density)


def solution(mesh):
    n_aux, n_occ = mesh.shape["aux"], mesh.shape["occ"]
    fetch = n_aux == 2 * 2 and n_occ & (n_occ - 1) == 0
    return jax.shard_map(
        pair_shards if fetch else scatter_shards,
        mesh=mesh,
        in_specs=(P("aux", "occ", None), P("aux", "occ"), P("occ"), P(), P()),
        out_specs=(P(("occ", "aux"), None), P("aux", "occ", None)),
        check_vma=False,
    )
```

```python
import jax
import jax.numpy as jnp
from jax import lax
from jax.experimental import pallas as pl
from jax.experimental.pallas import tpu as pltpu
from jax.sharding import PartitionSpec as P

BF16 = jnp.bfloat16
F32 = jnp.float32


def lookup(entries, indices):
    positions = jnp.arange(entries.shape[0], dtype=jnp.int32)
    matches = indices[:, None] == positions[None, :]
    return jnp.sum(jnp.where(matches, entries[None, :], 0.0), axis=1)


def scatter_shards(factors, partner, occupied_energy, partner_energy, virtual_energy):
    aux_rows, local_occ, virt_count = factors.shape
    partner_full = lax.all_gather(partner, "occ", axis=1, tiled=True)
    flat_factors = factors.reshape(aux_rows, local_occ * virt_count)
    total_rows = local_occ * virt_count
    row_share = total_rows // lax.axis_size("aux")
    own_first = lax.axis_index("aux") * row_share
    integrals = lax.psum_scatter(
        lax.dot_general(flat_factors, partner_full, (((0,), (0,)), ((), ())), preferred_element_type=F32).astype(BF16),
        "aux",
        scatter_dimension=0,
        tiled=True,
    ).astype(F32)
    row_ids = own_first + jnp.arange(row_share, dtype=jnp.int32)
    occ_part = lookup(occupied_energy, row_ids // virt_count)
    virt_part = lookup(virtual_energy, row_ids % virt_count)
    divisor = virt_part[:, None] + virtual_energy[None, :] - occ_part[:, None] - partner_energy[0]
    amp_shard = (-integrals / divisor).astype(BF16)
    amp_full = lax.all_gather(amp_shard, "aux", axis=0, tiled=True)
    amp_cube = amp_full.reshape(local_occ, virt_count, virt_count)
    direct = jnp.einsum("qb,iab->qia", partner_full, amp_cube, preferred_element_type=F32)
    swapped = jnp.einsum("qb,iba->qia", partner_full, amp_cube, preferred_element_type=F32)
    density = (2.0 * direct - swapped).astype(BF16)
    return (amp_shard, density)


MIB = 1024 * 1024


SCALAR = pl.BlockSpec(memory_space=pltpu.SMEM)
WHOLE = pl.BlockSpec(memory_space=pltpu.VMEM)
UNREAD = pl.BlockSpec(memory_space=pl.ANY)
LANES = 128


def kernel(body, name, mib, out, inputs, unread=(), scratch=(), grid=None, out_specs=None):
    count = len(inputs)

    def without_unread(*refs):
        body(*refs[:count], *refs[count + len(unread) :])

    return pl.pallas_call(
        without_unread,
        grid=grid or (),
        in_specs=[SCALAR] + [WHOLE] * (count - 1) + [UNREAD] * len(unread),
        out_specs=out_specs or jax.tree.map(lambda _: WHOLE, out),
        out_shape=out,
        scratch_shapes=list(scratch),
        compiler_params=pltpu.CompilerParams(vmem_limit_bytes=mib * 1024 * 1024),
        cost_estimate=pl.CostEstimate(flops=1, bytes_accessed=1, transcendentals=0),
        name=name,
    )(*inputs, *unread)


def shaped(shape, dtype=BF16):
    return jax.ShapeDtypeStruct(shape, dtype)


def turn(places, near_shard, far_shard, energies, virtual_energy):
    aux_rows, width = near_shard.shape
    virt_count = virtual_energy.shape[1]

    def body(places_ref, a_ref, b_ref, energies_ref, virtual_ref, out_ref, rows_ref, columns_ref):
        out_ref[0] = a_ref[...].T
        out_ref[1] = b_ref[...].T
        rows_ref[...] = jnp.broadcast_to(virtual_ref[...], (LANES, virt_count)).T
        first, second = energies_ref[:, 0:1], energies_ref[:, 1:2]
        near = places_ref[0] == 1
        virtual = virtual_ref[...] - energies_ref[:, 2:3]
        columns_ref[:, :virt_count] = virtual - jnp.where(near, second, first)
        columns_ref[:, virt_count:] = virtual - jnp.where(near, first, second)

    out = [shaped((2, width, aux_rows)), shaped((virt_count, LANES), F32), shaped((1, 2 * virt_count), F32)]
    return kernel(body, "turn_shards", 8, out, (places, near_shard, far_shard, energies, virtual_energy))


def pick(places, flat, spans, *unread):
    aux_rows, width = flat.shape
    unit = width // 8

    def body(places_ref, flat_ref, *out_refs):
        shift = jnp.where(places_ref[0] == 1, 0, width // 2)
        for (first, last), out_ref in zip(spans, out_refs, strict=True):
            for at in range(first, last, unit):
                source = lax.rem(at + shift, width)
                out_ref[:, at - first : at - first + unit] = flat_ref[:, pl.ds(pl.multiple_of(source, unit), unit)]

    return kernel(body, "pick_pieces", 8, [shaped((aux_rows, b - a)) for a, b in spans], (places, flat), unread)


def stack_blocks(places, blocks, *unread):
    def body(places_ref, *refs):
        for n, ref in enumerate(refs[:-1]):
            refs[-1][n] = ref[...]

    return kernel(body, "stack_blocks", 8, shaped((len(blocks),) + blocks[0].shape), (places, *blocks), unread)


def assemble(places, blocks, swapped, *unread):
    _, width, aux_rows = blocks[0].shape
    count = len(blocks)
    virt_count = 2 * width * count

    def body(places_ref, *refs):
        own_t_ref, far_t_ref, own_ref = refs[-3:]
        at = [ref.at[n] for ref in refs[count:-3] for n in range(ref.shape[0])]
        for k, ref in enumerate([ref for pair in zip(refs[:count], at, strict=True) for ref in pair]):
            first = pl.multiple_of((places_ref[2] ^ k) * width, width)
            own_t_ref[pl.ds(first, width), :] = ref[0]
            far_t_ref[pl.ds(first, width), :] = ref[1]
            own_ref[:, pl.ds(first, width)] = ref[0].T

    out = [shaped((virt_count, aux_rows))] * 2 + [shaped((aux_rows, virt_count))]
    return kernel(body, "assemble_partner", 12, out, (places, *blocks, *swapped), unread)


def dot_rows(own, amp):
    return jnp.dot(own, amp, preferred_element_type=F32)


def dot_columns(own, amp):
    return lax.dot_general(own, amp, (((1,), (1,)), ((), ())), preferred_element_type=F32)


def partial_integrals(places, own_t, far_t, flat, fetched, first, *unread):
    virt_count = own_t.shape[0]
    width, share = flat.shape[1], fetched.shape[1]
    unit = width // 8

    def body(places_ref, own_ref, far_ref, flat_ref, fetched_ref, out_ref):
        shift = jnp.where(places_ref[0] == 1, width // 2, 0)
        for at in range(0, share, unit):
            source = pl.multiple_of(lax.rem(first + at + shift, width), unit)
            total = dot_rows(own_ref[...], flat_ref[:, pl.ds(source, unit)])
            total += dot_rows(far_ref[...], fetched_ref[:, at : at + unit])
            out_ref[:, at : at + unit] = total.astype(BF16)

    inputs = (places, own_t, far_t, flat, fetched)
    return kernel(body, "partial_integrals", 12, shaped((virt_count, share)), inputs, unread)


def amplitude_bands(rows_ref, columns_ref, first, part_ref, other_ref, out_ref):
    virt_count, share = part_ref.shape
    block = 32
    column = jnp.broadcast_to(columns_ref[:, first : first + share], (8, share))

    @pl.loop(0, virt_count // block, unroll=2)
    def _(r):
        band = pl.ds(pl.multiple_of(r * block, block), block)
        divisor = jnp.concatenate([rows_ref[band, :]] * (share // LANES), axis=1)
        divisor = divisor + jnp.concatenate([column] * (block // 8), axis=0)
        integrals = part_ref[band, :].astype(F32) + other_ref[band, :].astype(F32)
        inverse = pl.reciprocal(divisor, approx=True)
        inverse = inverse * (divisor * inverse - 2.0)
        out_ref[band, :] = (integrals * inverse).astype(BF16)


def amplitude_piece(places, rows, columns, first, part, other, *unread):
    def body(places_ref, rows_ref, columns_ref, part_ref, other_ref, out_ref):
        amplitude_bands(rows_ref, columns_ref, first, part_ref, other_ref, out_ref)

    return kernel(body, "amplitude_piece", 12, shaped(part.shape), (places, rows, columns, part, other), unread)


def clip_spans(spans, low, high):
    found = []
    for n, (first, last) in enumerate(spans):
        a, b = max(first, low), min(last, high)
        if a < b:
            found.append((n, a - first, a - low, b - low))
    return found


def own_amplitudes(places, amps, spans, virt_count, *unread):
    half, unit = virt_count // 2, virt_count // 4

    def body(places_ref, *refs):
        for core in range(2):

            @pl.when(places_ref[1] == core)
            def _():
                for n, skip, a, b in clip_spans(spans, core * half, (core + 1) * half):
                    for r in range(0, virt_count, unit):
                        refs[-1][a:b, r : r + unit] = refs[n][r : r + unit, skip : skip + b - a].T

    return kernel(body, "own_amplitudes", 12, shaped((half, virt_count)), (places, *amps), unread)


def add_terms(total, own_ref, amp_refs, found, at, unit):
    for n, skip, a, b in found:
        total = total - dot_columns(own_ref[:, a:b], amp_refs[n][at : at + unit, skip : skip + b - a])
    for n, skip, a, b in found:
        if a <= at < b:
            rows = own_ref[...]
            total = total + dot_rows(rows + rows, amp_refs[n][:, skip + at - a : skip + at - a + unit])
    return total


def density_terms(places, own, amps, found, dtype, *unread):
    aux_rows, virt_count = own.shape
    unit = virt_count // 4

    def body(places_ref, own_ref, *refs):
        for at in range(0, virt_count, unit):
            total = add_terms(jnp.zeros((aux_rows, unit), F32), own_ref, refs[:-1], found, at, unit)
            refs[-1][:, at : at + unit] = total.astype(dtype)

    return kernel(body, "density_terms", 16, shaped((aux_rows, virt_count), dtype), (places, own, *amps), unread)


def finish(places, rows, columns, first, part, other, own, earlier, near_density, *unread):
    virt_count, share = part.shape
    aux_rows = own.shape[0]
    unit, block = virt_count // 4, aux_rows // 8
    found = [(0, 0, virt_count - share, virt_count)]

    def body(places_ref, rows_ref, columns_ref, part_ref, other_ref, own_ref, earlier_ref, ready_ref, out_ref, amp_ref, density_ref):
        step = pl.program_id(0)

        @pl.when(step == 0)
        def _():
            amplitude_bands(rows_ref, columns_ref, first, part_ref, other_ref, amp_ref)
            for at in range(0, virt_count, unit):
                total = add_terms(earlier_ref[:, at : at + unit], own_ref, [amp_ref], found, at, unit)
                density_ref[:, at : at + unit] = total.astype(BF16)

        band = pl.ds(pl.multiple_of(step * block, block), block)
        density, ready = density_ref[band, :], ready_ref[band, :]
        swap = places_ref[0] == 1
        out_ref[:, 0, :] = jnp.where(swap, density, ready)
        out_ref[:, 1, :] = jnp.where(swap, ready, density)

    return kernel(
        body,
        "finish_density",
        20,
        shaped((aux_rows, 2, virt_count)),
        (places, rows, columns, part, other, own, earlier, near_density),
        unread,
        scratch=[pltpu.VMEM(part.shape, BF16), pltpu.VMEM((aux_rows, virt_count), BF16)],
        grid=(aux_rows // block,),
        out_specs=pl.BlockSpec((block, 2, virt_count), lambda n: (n, 0, 0)),
    )


def pair_shards(factors, partner, occupied_energy, partner_energy, virtual_energy):
    aux_rows, local_occ, virt_count = factors.shape
    n_aux = lax.axis_size("aux")
    n_occ = lax.axis_size("occ")
    width, unit = local_occ * virt_count, virt_count // 4
    across = [(d, (d + n_aux // 2) % n_aux) for d in range(n_aux)]
    within = [(d, d ^ 1) for d in range(n_aux)]
    place = lax.axis_index("aux")
    places = jnp.stack([place // 2, place % 2, lax.axis_index("occ")]).astype(jnp.int32)
    energies = jnp.concatenate([occupied_energy, partner_energy]).reshape(1, local_occ + 1)
    places, energies, partner, factors = lax.optimization_barrier((places, energies, partner, factors))

    def occ_swap(value, k):
        return lax.ppermute(value, "occ", [(d, d ^ k) for d in range(n_occ)])

    far = lax.ppermute(partner, "aux", across)
    flat = factors.reshape(aux_rows, width)
    edges = [n * unit for n in (0, 2, 3, 5, 6, 8)]
    spans = list(zip(edges[:-1], edges[1:], strict=True))
    sent = pick(places, flat, spans[:1], far)
    sent += pick(places, flat, spans[1:], sent[0])
    fetched = [lax.ppermute(piece, "aux", across) for piece in sent]

    shard, rows, columns = turn(places, partner, far, energies, virtual_energy.reshape(1, virt_count))
    by_2, by_4 = occ_swap(shard, 2), occ_swap(shard, 4)
    by_1 = occ_swap(stack_blocks(places, (shard, by_2)), 1)
    (by_4,) = jnp.split(stack_blocks(places, (by_4,), fetched[0]), 1)
    by_4 = by_4.reshape(shard.shape)
    by_6 = occ_swap(by_4, 2)
    by_5 = occ_swap(stack_blocks(places, (by_4, by_6), by_1, fetched[1]), 1)
    own_t, far_t, own = assemble(places, (shard, by_2, by_4, by_6), (by_1, by_5), fetched[2])

    def partial(n, *unread):
        return partial_integrals(places, own_t, far_t, flat, fetched[n], spans[n][0], *unread)

    def amplitudes(n, part, *unread):
        return amplitude_piece(places, rows, columns, spans[n][0], part, lax.ppermute(part, "aux", within), *unread)

    parts = [partial(0)]
    for n in range(1, 4):
        parts.append(partial(n, parts[-1]))
    amps = [amplitudes(n, parts[n], parts[3]) for n in range(4)]
    near_density = density_terms(places, own, amps[:3], clip_spans(spans[:3], 0, virt_count), BF16)
    earlier = density_terms(places, own, amps, clip_spans(spans[:4], virt_count, width), F32)
    part = partial(4, near_density, earlier)
    other = lax.ppermute(part, "aux", within)
    amp_shard = own_amplitudes(places, amps[:3], spans[:3], virt_count, part)
    density = finish(places, rows, columns, spans[4][0], part, other, own, earlier, near_density, amp_shard)
    return (amp_shard, density)


def solution(mesh):
    n_aux, n_occ = mesh.shape["aux"], mesh.shape["occ"]
    fetch = n_aux == 2 * 2 and n_occ == 2 * 2 * 2
    return jax.shard_map(
        pair_shards if fetch else scatter_shards,
        mesh=mesh,
        in_specs=(P("aux", "occ", None), P("aux", "occ"), P("occ"), P(), P()),
        out_specs=(P(("occ", "aux"), None), P("aux", "occ", None)),
        check_vma=False,
    )
```

```python
import jax
import jax.numpy as jnp
from jax import lax
from jax.experimental import pallas as pl
from jax.experimental.pallas import tpu as pltpu
from jax.sharding import PartitionSpec as P

BF16 = jnp.bfloat16
F32 = jnp.float32


def lookup(entries, indices):
    positions = jnp.arange(entries.shape[0], dtype=jnp.int32)
    matches = indices[:, None] == positions[None, :]
    return jnp.sum(jnp.where(matches, entries[None, :], 0.0), axis=1)


def scatter_shards(factors, partner, occupied_energy, partner_energy, virtual_energy):
    aux_rows, local_occ, virt_count = factors.shape
    partner_full = lax.all_gather(partner, "occ", axis=1, tiled=True)
    flat_factors = factors.reshape(aux_rows, local_occ * virt_count)
    total_rows = local_occ * virt_count
    row_share = total_rows // lax.axis_size("aux")
    own_first = lax.axis_index("aux") * row_share
    integrals = lax.psum_scatter(
        lax.dot_general(flat_factors, partner_full, (((0,), (0,)), ((), ())), preferred_element_type=F32).astype(BF16),
        "aux",
        scatter_dimension=0,
        tiled=True,
    ).astype(F32)
    row_ids = own_first + jnp.arange(row_share, dtype=jnp.int32)
    occ_part = lookup(occupied_energy, row_ids // virt_count)
    virt_part = lookup(virtual_energy, row_ids % virt_count)
    divisor = virt_part[:, None] + virtual_energy[None, :] - occ_part[:, None] - partner_energy[0]
    amp_shard = (-integrals / divisor).astype(BF16)
    amp_full = lax.all_gather(amp_shard, "aux", axis=0, tiled=True)
    amp_cube = amp_full.reshape(local_occ, virt_count, virt_count)
    direct = jnp.einsum("qb,iab->qia", partner_full, amp_cube, preferred_element_type=F32)
    swapped = jnp.einsum("qb,iba->qia", partner_full, amp_cube, preferred_element_type=F32)
    density = (2.0 * direct - swapped).astype(BF16)
    return (amp_shard, density)


MIB = 1024 * 1024


WHOLE = pl.BlockSpec(memory_space=pltpu.VMEM)
UNREAD = pl.BlockSpec(memory_space=pl.ANY)
LANES = 128


def kernel(body, name, mib, out, inputs, unread=(), scratch=(), grid=None, out_specs=None):
    count = len(inputs)

    def without_unread(*refs):
        body(*refs[:count], *refs[count + len(unread) :])

    return pl.pallas_call(
        without_unread,
        grid=grid or (),
        in_specs=[WHOLE] * count + [UNREAD] * len(unread),
        out_specs=out_specs or jax.tree.map(lambda _: WHOLE, out),
        out_shape=out,
        scratch_shapes=list(scratch),
        compiler_params=pltpu.CompilerParams(vmem_limit_bytes=mib * 1024 * 1024),
        cost_estimate=pl.CostEstimate(flops=1, bytes_accessed=1, transcendentals=0),
        name=name,
    )(*inputs, *unread)


def shaped(shape, dtype=BF16):
    return jax.ShapeDtypeStruct(shape, dtype)


def turn(near_shard, far_shard, occupied_energy, partner_energy, virtual_energy, *unread):
    aux_rows, width = near_shard.shape
    virt_count = virtual_energy.shape[1]

    def body(a_ref, b_ref, occupied_ref, partner_ref, virtual_ref, out_ref, rows_ref, columns_ref):
        out_ref[0] = a_ref[...].T
        out_ref[1] = b_ref[...].T
        rows_ref[...] = jnp.broadcast_to(virtual_ref[...], (LANES, virt_count)).T
        first, second = occupied_ref[:, 0:1], occupied_ref[:, 1:2]
        near = near_place() == 1
        virtual = virtual_ref[...] - partner_ref[...]
        columns_ref[:, :virt_count] = virtual - jnp.where(near, second, first)
        columns_ref[:, virt_count:] = virtual - jnp.where(near, first, second)

    out = [shaped((2, width, aux_rows)), shaped((virt_count, LANES), F32), shaped((1, 2 * virt_count), F32)]
    inputs = (near_shard, far_shard, occupied_energy, partner_energy, virtual_energy)
    return kernel(body, "turn_shards", 8, out, inputs, unread)


def pick(flat, spans, *unread):
    aux_rows, width = flat.shape
    unit = width // 8

    def body(flat_ref, *out_refs):
        shift = jnp.where(near_place() == 1, 0, width // 2)
        for (first, last), out_ref in zip(spans, out_refs, strict=True):
            for at in range(first, last, unit):
                source = lax.rem(at + shift, width)
                out_ref[:, at - first : at - first + unit] = flat_ref[:, pl.ds(pl.multiple_of(source, unit), unit)]

    return kernel(body, "pick_pieces", 8, [shaped((aux_rows, b - a)) for a, b in spans], (flat,), unread)


def held(block, *unread):
    def body(block_ref, out_ref):
        out_ref[...] = block_ref[...]

    return kernel(body, "held_block", 8, shaped(block.shape), (block,), unread)


def assemble(blocks):
    _, width, aux_rows = blocks[0].shape
    virt_count = width * len(blocks)

    def body(*refs):
        own_t_ref, far_t_ref, own_ref = refs[-3:]
        for k, ref in enumerate(refs[:-3]):
            first = pl.multiple_of((lax.axis_index("occ") ^ k) * width, width)
            own_t_ref[pl.ds(first, width), :] = ref[0]
            far_t_ref[pl.ds(first, width), :] = ref[1]
            own_ref[:, pl.ds(first, width)] = ref[0].T

    out = [shaped((virt_count, aux_rows))] * 2 + [shaped((aux_rows, virt_count))]
    return kernel(body, "assemble_partner", 12, out, tuple(blocks))


def near_place():
    return lax.axis_index("aux") // 2


def core_place():
    return lax.axis_index("aux") % 2


def dot_rows(own, amp):
    return jnp.dot(own, amp, preferred_element_type=F32)


def dot_columns(own, amp):
    return lax.dot_general(own, amp, (((1,), (1,)), ((), ())), preferred_element_type=F32)


def partial_integrals(own_t, far_t, flat, fetched, first, *unread):
    virt_count = own_t.shape[0]
    width, share = flat.shape[1], fetched.shape[1]
    unit = width // 8

    def body(own_ref, far_ref, flat_ref, fetched_ref, *out_refs):
        shift = jnp.where(near_place() == 1, width // 2, 0)
        for n, out_ref in enumerate(out_refs):
            source = pl.multiple_of(lax.rem(first + n * unit + shift, width), unit)
            total = dot_rows(own_ref[...], flat_ref[:, pl.ds(source, unit)])
            total += dot_rows(far_ref[...], fetched_ref[:, n * unit : (n + 1) * unit])
            out_ref[...] = total.astype(BF16)

    out = [shaped((virt_count, unit))] * (share // unit)
    return kernel(body, "partial_integrals", 12, out, (own_t, far_t, flat, fetched), unread)


def amplitude_bands(rows_ref, columns_ref, first, part_refs, other_refs, out_ref):
    virt_count, unit = part_refs[0].shape
    block = 32

    for n, (part_ref, other_ref) in enumerate(zip(part_refs, other_refs, strict=True)):
        at = slice(n * unit, (n + 1) * unit)
        column = jnp.broadcast_to(columns_ref[:, first + n * unit : first + (n + 1) * unit], (8, unit))

        @pl.loop(0, virt_count // block, unroll=2)
        def _(r, at=at, column=column, part_ref=part_ref, other_ref=other_ref):
            band = pl.ds(pl.multiple_of(r * block, block), block)
            divisor = jnp.concatenate([rows_ref[band, :]] * (unit // LANES), axis=1)
            divisor = divisor + jnp.concatenate([column] * (block // 8), axis=0)
            integrals = part_ref[band, :].astype(F32) + other_ref[band, :].astype(F32)
            inverse = pl.reciprocal(divisor, approx=True)
            inverse = inverse * (divisor * inverse - 2.0)
            out_ref[band, at] = (integrals * inverse).astype(BF16)


def amplitude_piece(rows, columns, first, parts, others, *unread):
    count = len(parts)
    virt_count, unit = parts[0].shape

    def body(rows_ref, columns_ref, *refs):
        amplitude_bands(rows_ref, columns_ref, first, refs[:count], refs[count:-1], refs[-1])

    out = shaped((virt_count, count * unit))
    return kernel(body, "amplitude_piece", 12, out, (rows, columns, *parts, *others), unread)


def clip_spans(spans, low, high):
    found = []
    for n, (first, last) in enumerate(spans):
        a, b = max(first, low), min(last, high)
        if a < b:
            found.append((n, a - first, a - low, b - low))
    return found


def own_amplitudes(amps, spans, virt_count, *unread):
    half, unit = virt_count // 2, virt_count // 4

    def body(*refs):
        for core in range(2):

            @pl.when(core_place() == core)
            def _():
                for n, skip, a, b in clip_spans(spans, core * half, (core + 1) * half):
                    for r in range(0, virt_count, unit):
                        refs[-1][a:b, r : r + unit] = refs[n][r : r + unit, skip : skip + b - a].T

    return kernel(body, "own_amplitudes", 12, shaped((half, virt_count)), tuple(amps), unread)


def add_terms(total, own_ref, amp_refs, found, at, unit):
    for n, skip, a, b in found:
        total = total - dot_columns(own_ref[:, a:b], amp_refs[n][at : at + unit, skip : skip + b - a])
    for n, skip, a, b in found:
        if a <= at < b:
            rows = own_ref[...]
            total = total + dot_rows(rows + rows, amp_refs[n][:, skip + at - a : skip + at - a + unit])
    return total


def density_terms(own, amps, found, dtype, *unread):
    aux_rows, virt_count = own.shape
    unit = virt_count // 4

    def body(own_ref, *refs):
        for at in range(0, virt_count, unit):
            total = add_terms(jnp.zeros((aux_rows, unit), F32), own_ref, refs[:-1], found, at, unit)
            refs[-1][:, at : at + unit] = total.astype(dtype)

    return kernel(body, "density_terms", 16, shaped((aux_rows, virt_count), dtype), (own, *amps), unread)


def finish(rows, columns, first, parts, others, own, earlier, near_density):
    count = len(parts)
    virt_count, unit = parts[0].shape
    aux_rows, share = own.shape[0], count * unit
    block = aux_rows // 2
    found = [(0, 0, virt_count - share, virt_count)]

    def body(rows_ref, columns_ref, *refs):
        part_refs, other_refs = refs[:count], refs[count : 2 * count]
        own_ref, earlier_ref, ready_ref, out_ref, amp_ref, density_ref = refs[2 * count :]
        step = pl.program_id(0)

        @pl.when(step == 0)
        def _():
            amplitude_bands(rows_ref, columns_ref, first, part_refs, other_refs, amp_ref)
            for at in range(0, virt_count, unit):
                total = add_terms(earlier_ref[:, at : at + unit], own_ref, [amp_ref], found, at, unit)
                density_ref[:, at : at + unit] = total.astype(BF16)

        band = pl.ds(pl.multiple_of(step * block, block), block)
        density, ready = density_ref[band, :], ready_ref[band, :]
        swap = near_place() == 1
        out_ref[:, 0, :] = jnp.where(swap, density, ready)
        out_ref[:, 1, :] = jnp.where(swap, ready, density)

    return kernel(
        body,
        "finish_density",
        20,
        shaped((aux_rows, 2, virt_count)),
        (rows, columns, *parts, *others, own, earlier, near_density),
        scratch=[pltpu.VMEM((virt_count, share), BF16), pltpu.VMEM((aux_rows, virt_count), BF16)],
        grid=(aux_rows // block,),
        out_specs=pl.BlockSpec((block, 2, virt_count), lambda n: (n, 0, 0)),
    )


def pair_shards(factors, partner, occupied_energy, partner_energy, virtual_energy):
    aux_rows, local_occ, virt_count = factors.shape
    n_aux = lax.axis_size("aux")
    n_occ = lax.axis_size("occ")
    width, unit = local_occ * virt_count, virt_count // 4
    across = [(d, (d + n_aux // 2) % n_aux) for d in range(n_aux)]
    within = [(d, d ^ 1) for d in range(n_aux)]
    def occ_swap(value, k):
        return lax.ppermute(value, "occ", [(d, d ^ k) for d in range(n_occ)])

    far = lax.ppermute(partner, "aux", across)
    flat = factors.reshape(aux_rows, width)
    edges = [n * unit for n in (0, 1, 2, 3, 6, 8)]
    spans = list(zip(edges[:-1], edges[1:], strict=True))
    last = len(spans) - 1
    sent = pick(flat, spans[:1])
    sent += pick(flat, spans[1:], sent[0])
    fetched = [lax.ppermute(piece, "aux", across) for piece in sent]

    line = virtual_energy.reshape(1, virt_count)
    occupied, resident = occupied_energy.reshape(1, local_occ), partner_energy.reshape(1, 1)
    shard, rows, columns = turn(partner, far, occupied, resident, line, sent[0])
    by_4 = occ_swap(shard, 4)
    by_2 = occ_swap(shard, 2)
    by_1 = occ_swap(shard, 1)
    by_3 = occ_swap(held(by_2, by_1, fetched[0]), 1)
    by_4 = held(by_4, by_3, fetched[1])
    by_6 = occ_swap(by_4, 2)
    by_5 = occ_swap(by_4, 1)
    by_7 = occ_swap(held(by_6, by_5, fetched[2]), 1)
    own_t, far_t, own = assemble([shard, by_1, by_2, by_3, by_4, by_5, by_6, by_7])

    def partial(n, *unread):
        return partial_integrals(own_t, far_t, flat, fetched[n], spans[n][0], *unread)

    def other_core(parts):
        return [lax.ppermute(part, "aux", within) for part in parts]

    parts = [partial(0)]
    for n in range(1, 3):
        parts.append(partial(n, parts[-1][0]))
    amps = [amplitude_piece(rows, columns, spans[n][0], parts[n], other_core(parts[n])) for n in range(3)]
    third = partial(3, *amps)
    amps.append(amplitude_piece(rows, columns, spans[3][0], third, other_core(third)))
    near_density = density_terms(own, amps, clip_spans(spans[:last], 0, virt_count), BF16)
    earlier = density_terms(own, amps, clip_spans(spans[:last], virt_count, width), F32, near_density)
    parts = partial(last, earlier)
    others = other_core(parts)
    amp_shard = own_amplitudes(amps, spans[:last], virt_count, parts[0])
    density = finish(rows, columns, spans[last][0], parts, others, own, earlier, near_density)
    return (amp_shard, density)


def solution(mesh):
    n_aux, n_occ = mesh.shape["aux"], mesh.shape["occ"]
    fetch = n_aux == 2 * 2 and n_occ == 2 * 2 * 2
    return jax.shard_map(
        pair_shards if fetch else scatter_shards,
        mesh=mesh,
        in_specs=(P("aux", "occ", None), P("aux", "occ"), P("occ"), P(), P()),
        out_specs=(P(("occ", "aux"), None), P("aux", "occ", None)),
        check_vma=False,
    )
```

```python
import jax
import jax.numpy as jnp
from jax import lax
from jax.experimental import pallas as pl
from jax.experimental.pallas import tpu as pltpu
from jax.sharding import PartitionSpec as P

BF16 = jnp.bfloat16
F32 = jnp.float32


def lookup(entries, indices):
    positions = jnp.arange(entries.shape[0], dtype=jnp.int32)
    matches = indices[:, None] == positions[None, :]
    return jnp.sum(jnp.where(matches, entries[None, :], 0.0), axis=1)


def scatter_shards(factors, partner, occupied_energy, partner_energy, virtual_energy):
    aux_rows, local_occ, virt_count = factors.shape
    partner_full = lax.all_gather(partner, "occ", axis=1, tiled=True)
    flat_factors = factors.reshape(aux_rows, local_occ * virt_count)
    total_rows = local_occ * virt_count
    row_share = total_rows // lax.axis_size("aux")
    own_first = lax.axis_index("aux") * row_share
    integrals = lax.psum_scatter(
        lax.dot_general(flat_factors, partner_full, (((0,), (0,)), ((), ())), preferred_element_type=F32).astype(BF16),
        "aux",
        scatter_dimension=0,
        tiled=True,
    ).astype(F32)
    row_ids = own_first + jnp.arange(row_share, dtype=jnp.int32)
    occ_part = lookup(occupied_energy, row_ids // virt_count)
    virt_part = lookup(virtual_energy, row_ids % virt_count)
    divisor = virt_part[:, None] + virtual_energy[None, :] - occ_part[:, None] - partner_energy[0]
    amp_shard = (-integrals / divisor).astype(BF16)
    amp_full = lax.all_gather(amp_shard, "aux", axis=0, tiled=True)
    amp_cube = amp_full.reshape(local_occ, virt_count, virt_count)
    direct = jnp.einsum("qb,iab->qia", partner_full, amp_cube, preferred_element_type=F32)
    swapped = jnp.einsum("qb,iba->qia", partner_full, amp_cube, preferred_element_type=F32)
    density = (2.0 * direct - swapped).astype(BF16)
    return (amp_shard, density)


MIB = 1024 * 1024


WHOLE = pl.BlockSpec(memory_space=pltpu.VMEM)
UNREAD = pl.BlockSpec(memory_space=pl.ANY)
LANES = 128


def kernel(body, name, mib, out, inputs, unread=(), scratch=(), grid=None, out_specs=None):
    count = len(inputs)

    def without_unread(*refs):
        body(*refs[:count], *refs[count + len(unread) :])

    return pl.pallas_call(
        without_unread,
        grid=grid or (),
        in_specs=[WHOLE] * count + [UNREAD] * len(unread),
        out_specs=out_specs or jax.tree.map(lambda _: WHOLE, out),
        out_shape=out,
        scratch_shapes=list(scratch),
        compiler_params=pltpu.CompilerParams(vmem_limit_bytes=mib * 1024 * 1024),
        cost_estimate=pl.CostEstimate(flops=1, bytes_accessed=1, transcendentals=0),
        name=name,
    )(*inputs, *unread)


def shaped(shape, dtype=BF16):
    return jax.ShapeDtypeStruct(shape, dtype)


def turn(near_shard, far_shard, occupied_energy, partner_energy, virtual_energy, *unread):
    aux_rows, width = near_shard.shape
    virt_count = virtual_energy.shape[1]

    def body(a_ref, b_ref, occupied_ref, partner_ref, virtual_ref, out_ref, rows_ref, columns_ref):
        out_ref[0] = a_ref[...].T
        out_ref[1] = b_ref[...].T
        rows_ref[...] = jnp.broadcast_to(virtual_ref[...], (LANES, virt_count)).T
        first, second = occupied_ref[:, 0:1], occupied_ref[:, 1:2]
        near = near_place() == 1
        virtual = virtual_ref[...] - partner_ref[...]
        columns_ref[:, :virt_count] = virtual - jnp.where(near, second, first)
        columns_ref[:, virt_count:] = virtual - jnp.where(near, first, second)

    out = [shaped((2, width, aux_rows)), shaped((virt_count, LANES), F32), shaped((1, 2 * virt_count), F32)]
    inputs = (near_shard, far_shard, occupied_energy, partner_energy, virtual_energy)
    return kernel(body, "turn_shards", 8, out, inputs, unread)


def pick(flat, spans, *unread):
    aux_rows, width = flat.shape
    unit = width // 8

    def body(flat_ref, *out_refs):
        shift = jnp.where(near_place() == 1, 0, width // 2)
        for (first, last), out_ref in zip(spans, out_refs, strict=True):
            for at in range(first, last, unit):
                source = lax.rem(at + shift, width)
                out_ref[:, at - first : at - first + unit] = flat_ref[:, pl.ds(pl.multiple_of(source, unit), unit)]

    return kernel(body, "pick_pieces", 8, [shaped((aux_rows, b - a)) for a, b in spans], (flat,), unread)


def held(block, *unread):
    def body(block_ref, out_ref):
        out_ref[...] = block_ref[...]

    return kernel(body, "held_block", 8, shaped(block.shape), (block,), unread)


def assemble(blocks):
    _, width, aux_rows = blocks[0].shape
    virt_count = width * len(blocks)

    def body(*refs):
        own_t_ref, far_t_ref, own_ref = refs[-3:]
        for k, ref in enumerate(refs[:-3]):
            first = pl.multiple_of((lax.axis_index("occ") ^ k) * width, width)
            own_t_ref[pl.ds(first, width), :] = ref[0]
            far_t_ref[pl.ds(first, width), :] = ref[1]
            own_ref[:, pl.ds(first, width)] = ref[0].T

    out = [shaped((virt_count, aux_rows))] * 2 + [shaped((aux_rows, virt_count))]
    return kernel(body, "assemble_partner", 12, out, tuple(blocks))


def near_place():
    return lax.axis_index("aux") // 2


def core_place():
    return lax.axis_index("aux") % 2


def dot_rows(own, amp):
    return jnp.dot(own, amp, preferred_element_type=F32)


def dot_columns(own, amp):
    return lax.dot_general(own, amp, (((1,), (1,)), ((), ())), preferred_element_type=F32)


def partial_integrals(own_t, far_t, flat, fetched, first, *unread):
    virt_count = own_t.shape[0]
    width, share = flat.shape[1], fetched.shape[1]
    unit = width // 8

    def body(own_ref, far_ref, flat_ref, fetched_ref, *out_refs):
        shift = jnp.where(near_place() == 1, width // 2, 0)
        for n, out_ref in enumerate(out_refs):
            source = pl.multiple_of(lax.rem(first + n * unit + shift, width), unit)
            total = dot_rows(own_ref[...], flat_ref[:, pl.ds(source, unit)])
            total += dot_rows(far_ref[...], fetched_ref[:, n * unit : (n + 1) * unit])
            out_ref[...] = total.astype(BF16)

    out = [shaped((virt_count, unit))] * (share // unit)
    return kernel(body, "partial_integrals", 12, out, (own_t, far_t, flat, fetched), unread)


def amplitude_bands(rows_ref, columns_ref, first, part_refs, other_refs, out_ref):
    virt_count, unit = part_refs[0].shape
    block = 32

    for n, (part_ref, other_ref) in enumerate(zip(part_refs, other_refs, strict=True)):
        at = slice(n * unit, (n + 1) * unit)
        column = jnp.broadcast_to(columns_ref[:, first + n * unit : first + (n + 1) * unit], (8, unit))

        @pl.loop(0, virt_count // block, unroll=2)
        def _(r, at=at, column=column, part_ref=part_ref, other_ref=other_ref):
            band = pl.ds(pl.multiple_of(r * block, block), block)
            divisor = jnp.concatenate([rows_ref[band, :]] * (unit // LANES), axis=1)
            divisor = divisor + jnp.concatenate([column] * (block // 8), axis=0)
            integrals = part_ref[band, :].astype(F32) + other_ref[band, :].astype(F32)
            inverse = pl.reciprocal(divisor, approx=True)
            inverse = inverse * (divisor * inverse - 2.0)
            out_ref[band, at] = (integrals * inverse).astype(BF16)


def amplitude_piece(rows, columns, first, parts, others, *unread):
    count = len(parts)
    virt_count, unit = parts[0].shape

    def body(rows_ref, columns_ref, *refs):
        amplitude_bands(rows_ref, columns_ref, first, refs[:count], refs[count:-1], refs[-1])

    out = shaped((virt_count, count * unit))
    return kernel(body, "amplitude_piece", 12, out, (rows, columns, *parts, *others), unread)


def clip_spans(spans, low, high):
    found = []
    for n, (first, last) in enumerate(spans):
        a, b = max(first, low), min(last, high)
        if a < b:
            found.append((n, a - first, a - low, b - low))
    return found


def own_amplitudes(amps, spans, virt_count, *unread):
    half, unit = virt_count // 2, virt_count // 4

    def body(*refs):
        for core in range(2):

            @pl.when(core_place() == core)
            def _():
                for n, skip, a, b in clip_spans(spans, core * half, (core + 1) * half):
                    for r in range(0, virt_count, unit):
                        refs[-1][a:b, r : r + unit] = refs[n][r : r + unit, skip : skip + b - a].T

    return kernel(body, "own_amplitudes", 12, shaped((half, virt_count)), tuple(amps), unread)


def add_terms(total, own_ref, amp_refs, found, at, unit):
    for n, skip, a, b in found:
        total = total - dot_columns(own_ref[:, a:b], amp_refs[n][at : at + unit, skip : skip + b - a])
    for n, skip, a, b in found:
        if a <= at < b:
            rows = own_ref[...]
            total = total + dot_rows(rows + rows, amp_refs[n][:, skip + at - a : skip + at - a + unit])
    return total


def density_terms(own, amps, found, dtype, *unread):
    aux_rows, virt_count = own.shape
    unit = virt_count // 4

    def body(own_ref, *refs):
        for at in range(0, virt_count, unit):
            total = add_terms(jnp.zeros((aux_rows, unit), F32), own_ref, refs[:-1], found, at, unit)
            refs[-1][:, at : at + unit] = total.astype(dtype)

    return kernel(body, "density_terms", 16, shaped((aux_rows, virt_count), dtype), (own, *amps), unread)


def finish(rows, columns, first, parts, others, own, earlier, near_density):
    count = len(parts)
    virt_count, unit = parts[0].shape
    aux_rows, share = own.shape[0], count * unit
    block = aux_rows // 2
    found = [(0, 0, virt_count - share, virt_count)]

    def body(rows_ref, columns_ref, *refs):
        part_refs, other_refs = refs[:count], refs[count : 2 * count]
        own_ref, earlier_ref, ready_ref, out_ref, amp_ref, density_ref = refs[2 * count :]
        step = pl.program_id(0)

        @pl.when(step == 0)
        def _():
            amplitude_bands(rows_ref, columns_ref, first, part_refs, other_refs, amp_ref)
            for at in range(0, virt_count, unit):
                total = add_terms(earlier_ref[:, at : at + unit], own_ref, [amp_ref], found, at, unit)
                density_ref[:, at : at + unit] = total.astype(BF16)

        band = pl.ds(pl.multiple_of(step * block, block), block)
        density, ready = density_ref[band, :], ready_ref[band, :]
        swap = near_place() == 1
        out_ref[:, 0, :] = jnp.where(swap, density, ready)
        out_ref[:, 1, :] = jnp.where(swap, ready, density)

    return kernel(
        body,
        "finish_density",
        20,
        shaped((aux_rows, 2, virt_count)),
        (rows, columns, *parts, *others, own, earlier, near_density),
        scratch=[pltpu.VMEM((virt_count, share), BF16), pltpu.VMEM((aux_rows, virt_count), BF16)],
        grid=(aux_rows // block,),
        out_specs=pl.BlockSpec((block, 2, virt_count), lambda n: (n, 0, 0)),
    )


def pair_shards(factors, partner, occupied_energy, partner_energy, virtual_energy):
    aux_rows, local_occ, virt_count = factors.shape
    n_aux = lax.axis_size("aux")
    n_occ = lax.axis_size("occ")
    width, unit = local_occ * virt_count, virt_count // 4
    across = [(d, (d + n_aux // 2) % n_aux) for d in range(n_aux)]
    within = [(d, d ^ 1) for d in range(n_aux)]
    def occ_swap(value, k):
        return lax.ppermute(value, "occ", [(d, d ^ k) for d in range(n_occ)])

    far = lax.ppermute(partner, "aux", across)
    flat = factors.reshape(aux_rows, width)
    edges = [n * unit for n in (0, 1, 2, 4, 7, 8)]
    spans = list(zip(edges[:-1], edges[1:], strict=True))
    last = len(spans) - 1
    sent = pick(flat, spans[:1])
    sent += pick(flat, spans[1:], sent[0])
    fetched = [lax.ppermute(piece, "aux", across) for piece in sent]

    line = virtual_energy.reshape(1, virt_count)
    occupied, resident = occupied_energy.reshape(1, local_occ), partner_energy.reshape(1, 1)
    shard, rows, columns = turn(partner, far, occupied, resident, line, sent[0])
    by_4 = occ_swap(shard, 4)
    by_2 = occ_swap(shard, 2)
    by_1 = occ_swap(shard, 1)
    by_3 = occ_swap(held(by_2, by_1, fetched[0]), 1)
    by_4 = held(by_4, by_3, fetched[1])
    by_6 = occ_swap(by_4, 2)
    by_5 = occ_swap(by_4, 1)
    by_7 = occ_swap(held(by_6, by_5, fetched[2]), 1)
    own_t, far_t, own = assemble([shard, by_1, by_2, by_3, by_4, by_5, by_6, by_7])

    def partial(n, *unread):
        return partial_integrals(own_t, far_t, flat, fetched[n], spans[n][0], *unread)

    def other_core(parts):
        return [lax.ppermute(part, "aux", within) for part in parts]

    parts = [partial(0)]
    for n in range(1, 3):
        parts.append(partial(n, parts[-1][0]))
    amps = [amplitude_piece(rows, columns, spans[n][0], parts[n], other_core(parts[n])) for n in range(3)]
    third = partial(3, *amps)
    near_density = density_terms(own, amps[:3], clip_spans(spans[:3], 0, virt_count), BF16, third[0])
    amps.append(amplitude_piece(rows, columns, spans[3][0], third, other_core(third), near_density))
    earlier = density_terms(own, amps[3:], clip_spans(spans[3:4], virt_count, width), F32)
    parts = partial(last, earlier)
    others = other_core(parts)
    amp_shard = own_amplitudes(amps[:3], spans[:3], virt_count, parts[0])
    density = finish(rows, columns, spans[last][0], parts, others, own, earlier, near_density)
    return (amp_shard, density)


def solution(mesh):
    n_aux, n_occ = mesh.shape["aux"], mesh.shape["occ"]
    fetch = n_aux == 2 * 2 and n_occ == 2 * 2 * 2
    return jax.shard_map(
        pair_shards if fetch else scatter_shards,
        mesh=mesh,
        in_specs=(P("aux", "occ", None), P("aux", "occ"), P("occ"), P(), P()),
        out_specs=(P(("occ", "aux"), None), P("aux", "occ", None)),
        check_vma=False,
    )
```

```python
import jax
import jax.numpy as jnp
from jax import lax
from jax.experimental import pallas as pl
from jax.experimental.pallas import tpu as pltpu
from jax.sharding import PartitionSpec as P

BF16 = jnp.bfloat16
F32 = jnp.float32


def lookup(entries, indices):
    positions = jnp.arange(entries.shape[0], dtype=jnp.int32)
    matches = indices[:, None] == positions[None, :]
    return jnp.sum(jnp.where(matches, entries[None, :], 0.0), axis=1)


def scatter_shards(factors, partner, occupied_energy, partner_energy, virtual_energy):
    aux_rows, local_occ, virt_count = factors.shape
    partner_full = lax.all_gather(partner, "occ", axis=1, tiled=True)
    flat_factors = factors.reshape(aux_rows, local_occ * virt_count)
    total_rows = local_occ * virt_count
    row_share = total_rows // lax.axis_size("aux")
    own_first = lax.axis_index("aux") * row_share
    integrals = lax.psum_scatter(
        lax.dot_general(flat_factors, partner_full, (((0,), (0,)), ((), ())), preferred_element_type=F32).astype(BF16),
        "aux",
        scatter_dimension=0,
        tiled=True,
    ).astype(F32)
    row_ids = own_first + jnp.arange(row_share, dtype=jnp.int32)
    occ_part = lookup(occupied_energy, row_ids // virt_count)
    virt_part = lookup(virtual_energy, row_ids % virt_count)
    divisor = virt_part[:, None] + virtual_energy[None, :] - occ_part[:, None] - partner_energy[0]
    amp_shard = (-integrals / divisor).astype(BF16)
    amp_full = lax.all_gather(amp_shard, "aux", axis=0, tiled=True)
    amp_cube = amp_full.reshape(local_occ, virt_count, virt_count)
    direct = jnp.einsum("qb,iab->qia", partner_full, amp_cube, preferred_element_type=F32)
    swapped = jnp.einsum("qb,iba->qia", partner_full, amp_cube, preferred_element_type=F32)
    density = (2.0 * direct - swapped).astype(BF16)
    return (amp_shard, density)


MIB = 1024 * 1024


WHOLE = pl.BlockSpec(memory_space=pltpu.VMEM)
UNREAD = pl.BlockSpec(memory_space=pl.ANY)
LANES = 128


def kernel(body, name, mib, out, inputs, unread=(), scratch=(), grid=None, out_specs=None):
    count = len(inputs)

    def without_unread(*refs):
        body(*refs[:count], *refs[count + len(unread) :])

    return pl.pallas_call(
        without_unread,
        grid=grid or (),
        in_specs=[WHOLE] * count + [UNREAD] * len(unread),
        out_specs=out_specs or jax.tree.map(lambda _: WHOLE, out),
        out_shape=out,
        scratch_shapes=list(scratch),
        compiler_params=pltpu.CompilerParams(vmem_limit_bytes=mib * 1024 * 1024),
        cost_estimate=pl.CostEstimate(flops=1, bytes_accessed=1, transcendentals=0),
        name=name,
    )(*inputs, *unread)


def shaped(shape, dtype=BF16):
    return jax.ShapeDtypeStruct(shape, dtype)


def turn(near_shard, far_shard, occupied_energy, partner_energy, virtual_energy, *unread):
    aux_rows, width = near_shard.shape
    virt_count = virtual_energy.shape[1]

    def body(a_ref, b_ref, occupied_ref, partner_ref, virtual_ref, out_ref, rows_ref, columns_ref):
        out_ref[0] = a_ref[...].T
        out_ref[1] = b_ref[...].T
        rows_ref[...] = jnp.broadcast_to(virtual_ref[...], (LANES, virt_count)).T
        first, second = occupied_ref[:, 0:1], occupied_ref[:, 1:2]
        near = near_place() == 1
        virtual = virtual_ref[...] - partner_ref[...]
        columns_ref[:, :virt_count] = virtual - jnp.where(near, second, first)
        columns_ref[:, virt_count:] = virtual - jnp.where(near, first, second)

    out = [shaped((2, width, aux_rows)), shaped((virt_count, LANES), F32), shaped((1, 2 * virt_count), F32)]
    inputs = (near_shard, far_shard, occupied_energy, partner_energy, virtual_energy)
    return kernel(body, "turn_shards", 8, out, inputs, unread)


def pick(flat, spans, *unread):
    aux_rows, width = flat.shape
    unit = width // 8

    def body(flat_ref, *out_refs):
        shift = jnp.where(near_place() == 1, 0, width // 2)
        for (first, last), out_ref in zip(spans, out_refs, strict=True):
            for at in range(first, last, unit):
                source = lax.rem(at + shift, width)
                out_ref[:, at - first : at - first + unit] = flat_ref[:, pl.ds(pl.multiple_of(source, unit), unit)]

    return kernel(body, "pick_pieces", 8, [shaped((aux_rows, b - a)) for a, b in spans], (flat,), unread)


def held(block, *unread):
    def body(block_ref, out_ref):
        out_ref[...] = block_ref[...]

    return kernel(body, "held_block", 8, shaped(block.shape), (block,), unread)


def assemble(blocks):
    _, width, aux_rows = blocks[0].shape
    virt_count = width * len(blocks)

    def body(*refs):
        own_t_ref, far_t_ref, own_ref = refs[-3:]
        for k, ref in enumerate(refs[:-3]):
            first = pl.multiple_of((lax.axis_index("occ") ^ k) * width, width)
            own_t_ref[pl.ds(first, width), :] = ref[0]
            far_t_ref[pl.ds(first, width), :] = ref[1]
            own_ref[:, pl.ds(first, width)] = ref[0].T

    out = [shaped((virt_count, aux_rows))] * 2 + [shaped((aux_rows, virt_count))]
    return kernel(body, "assemble_partner", 12, out, tuple(blocks))


def near_place():
    return lax.axis_index("aux") // 2


def core_place():
    return lax.axis_index("aux") % 2


def dot_rows(own, amp):
    return jnp.dot(own, amp, preferred_element_type=F32)


def dot_columns(own, amp):
    return lax.dot_general(own, amp, (((1,), (1,)), ((), ())), preferred_element_type=F32)


def partial_integrals(own_t, far_t, flat, fetched, first, *unread):
    virt_count = own_t.shape[0]
    width, share = flat.shape[1], fetched.shape[1]
    unit = width // 8

    def body(own_ref, far_ref, flat_ref, fetched_ref, *out_refs):
        shift = jnp.where(near_place() == 1, width // 2, 0)
        for n, out_ref in enumerate(out_refs):
            source = pl.multiple_of(lax.rem(first + n * unit + shift, width), unit)
            total = dot_rows(own_ref[...], flat_ref[:, pl.ds(source, unit)])
            total += dot_rows(far_ref[...], fetched_ref[:, n * unit : (n + 1) * unit])
            out_ref[...] = total.astype(BF16)

    out = [shaped((virt_count, unit))] * (share // unit)
    return kernel(body, "partial_integrals", 12, out, (own_t, far_t, flat, fetched), unread)


def amplitude_bands(rows_ref, columns_ref, first, part_refs, other_refs, out_ref):
    virt_count, unit = part_refs[0].shape
    block = 32

    for n, (part_ref, other_ref) in enumerate(zip(part_refs, other_refs, strict=True)):
        at = slice(n * unit, (n + 1) * unit)
        column = jnp.broadcast_to(columns_ref[:, first + n * unit : first + (n + 1) * unit], (8, unit))

        @pl.loop(0, virt_count // block, unroll=2)
        def _(r, at=at, column=column, part_ref=part_ref, other_ref=other_ref):
            band = pl.ds(pl.multiple_of(r * block, block), block)
            divisor = jnp.concatenate([rows_ref[band, :]] * (unit // LANES), axis=1)
            divisor = divisor + jnp.concatenate([column] * (block // 8), axis=0)
            integrals = part_ref[band, :].astype(F32) + other_ref[band, :].astype(F32)
            inverse = pl.reciprocal(divisor, approx=True)
            inverse = inverse * (divisor * inverse - 2.0)
            out_ref[band, at] = (integrals * inverse).astype(BF16)


def amplitude_piece(rows, columns, first, parts, others, *unread):
    count = len(parts)
    virt_count, unit = parts[0].shape

    def body(rows_ref, columns_ref, *refs):
        amplitude_bands(rows_ref, columns_ref, first, refs[:count], refs[count:-1], refs[-1])

    out = shaped((virt_count, count * unit))
    return kernel(body, "amplitude_piece", 12, out, (rows, columns, *parts, *others), unread)


def clip_spans(spans, low, high):
    found = []
    for n, (first, last) in enumerate(spans):
        a, b = max(first, low), min(last, high)
        if a < b:
            found.append((n, a - first, a - low, b - low))
    return found


def own_amplitudes(amps, spans, virt_count, *unread):
    half, unit = virt_count // 2, virt_count // 4

    def body(*refs):
        for core in range(2):

            @pl.when(core_place() == core)
            def _():
                for n, skip, a, b in clip_spans(spans, core * half, (core + 1) * half):
                    for r in range(0, virt_count, unit):
                        refs[-1][a:b, r : r + unit] = refs[n][r : r + unit, skip : skip + b - a].T

    return kernel(body, "own_amplitudes", 12, shaped((half, virt_count)), tuple(amps), unread)


def add_terms(total, own_ref, amp_refs, found, at, unit):
    for n, skip, a, b in found:
        total = total - dot_columns(own_ref[:, a:b], amp_refs[n][at : at + unit, skip : skip + b - a])
    for n, skip, a, b in found:
        if a <= at < b:
            rows = own_ref[...]
            total = total + dot_rows(rows + rows, amp_refs[n][:, skip + at - a : skip + at - a + unit])
    return total


def density_terms(own, amps, found, dtype, *unread):
    aux_rows, virt_count = own.shape
    unit = virt_count // 4

    def body(own_ref, *refs):
        for at in range(0, virt_count, unit):
            total = add_terms(jnp.zeros((aux_rows, unit), F32), own_ref, refs[:-1], found, at, unit)
            refs[-1][:, at : at + unit] = total.astype(dtype)

    return kernel(body, "density_terms", 16, shaped((aux_rows, virt_count), dtype), (own, *amps), unread)


def finish(rows, columns, first, parts, others, own, earlier, near_density):
    count = len(parts)
    virt_count, unit = parts[0].shape
    aux_rows, share = own.shape[0], count * unit
    block = aux_rows // 2
    found = [(0, 0, virt_count - share, virt_count)]

    def body(rows_ref, columns_ref, *refs):
        part_refs, other_refs = refs[:count], refs[count : 2 * count]
        own_ref, earlier_ref, ready_ref, out_ref, amp_ref, density_ref = refs[2 * count :]
        step = pl.program_id(0)

        @pl.when(step == 0)
        def _():
            amplitude_bands(rows_ref, columns_ref, first, part_refs, other_refs, amp_ref)
            for at in range(0, virt_count, unit):
                total = add_terms(earlier_ref[:, at : at + unit], own_ref, [amp_ref], found, at, unit)
                density_ref[:, at : at + unit] = total.astype(BF16)

        band = pl.ds(pl.multiple_of(step * block, block), block)
        density, ready = density_ref[band, :], ready_ref[band, :]
        swap = near_place() == 1
        out_ref[...] = jnp.stack([jnp.where(swap, density, ready), jnp.where(swap, ready, density)], axis=1)

    return kernel(
        body,
        "finish_density",
        20,
        shaped((aux_rows, 2, virt_count)),
        (rows, columns, *parts, *others, own, earlier, near_density),
        scratch=[pltpu.VMEM((virt_count, share), BF16), pltpu.VMEM((aux_rows, virt_count), BF16)],
        grid=(aux_rows // block,),
        out_specs=pl.BlockSpec((block, 2, virt_count), lambda n: (n, 0, 0)),
    )


def pair_shards(factors, partner, occupied_energy, partner_energy, virtual_energy):
    aux_rows, local_occ, virt_count = factors.shape
    n_aux = lax.axis_size("aux")
    n_occ = lax.axis_size("occ")
    width, unit = local_occ * virt_count, virt_count // 4
    across = [(d, (d + n_aux // 2) % n_aux) for d in range(n_aux)]
    within = [(d, d ^ 1) for d in range(n_aux)]
    def occ_swap(value, k):
        return lax.ppermute(value, "occ", [(d, d ^ k) for d in range(n_occ)])

    far = lax.ppermute(partner, "aux", across)
    flat = factors.reshape(aux_rows, width)
    edges = [n * unit for n in (0, 1, 3, 7, 8)]
    spans = list(zip(edges[:-1], edges[1:], strict=True))
    last = len(spans) - 1
    sent = pick(flat, spans[:1])
    sent += pick(flat, spans[1:], sent[0])
    fetched = [lax.ppermute(piece, "aux", across) for piece in sent]

    line = virtual_energy.reshape(1, virt_count)
    occupied, resident = occupied_energy.reshape(1, local_occ), partner_energy.reshape(1, 1)
    shard, rows, columns = turn(partner, far, occupied, resident, line, sent[0])
    by_4 = occ_swap(shard, 4)
    by_2 = occ_swap(shard, 2)
    by_1 = occ_swap(shard, 1)
    by_3 = occ_swap(held(by_2, by_1, fetched[0]), 1)
    by_4 = held(by_4, fetched[1])
    by_7 = occ_swap(by_3, 4)
    by_6 = occ_swap(by_4, 2)
    by_5 = occ_swap(by_4, 1)
    own_t, far_t, own = assemble([shard, by_1, by_2, by_3, by_4, by_5, by_6, by_7])

    def partial(n, *unread):
        return partial_integrals(own_t, far_t, flat, fetched[n], spans[n][0], *unread)

    def other_core(parts):
        return [lax.ppermute(part, "aux", within) for part in parts]

    def density_of(amps, low, high, dtype, *unread):
        return density_terms(own, amps, clip_spans(spans[:last], low, high), dtype, *unread)

    first = partial(0)
    second = partial(1, first[0])
    amps = [amplitude_piece(rows, columns, spans[n][0], p, other_core(p)) for n, p in enumerate((first, second))]
    third = partial(2, *amps)
    amps.append(amplitude_piece(rows, columns, spans[2][0], third, other_core(third)))
    near_density = density_of(amps, 0, virt_count, BF16)
    earlier = density_of(amps, virt_count, width, F32, near_density)
    parts = partial(last, earlier)
    others = other_core(parts)
    amp_shard = own_amplitudes(amps, spans[:last], virt_count, parts[0])
    density = finish(rows, columns, spans[last][0], parts, others, own, earlier, near_density)
    return (amp_shard, density)


def solution(mesh):
    n_aux, n_occ = mesh.shape["aux"], mesh.shape["occ"]
    fetch = n_aux == 2 * 2 and n_occ == 2 * 2 * 2
    return jax.shard_map(
        pair_shards if fetch else scatter_shards,
        mesh=mesh,
        in_specs=(P("aux", "occ", None), P("aux", "occ"), P("occ"), P(), P()),
        out_specs=(P(("occ", "aux"), None), P("aux", "occ", None)),
        check_vma=False,
    )
```

```python
import jax
import jax.numpy as jnp
from jax import lax
from jax.experimental import pallas as pl
from jax.experimental.pallas import tpu as pltpu
from jax.sharding import PartitionSpec as P

BF16 = jnp.bfloat16
F32 = jnp.float32


def lookup(entries, indices):
    positions = jnp.arange(entries.shape[0], dtype=jnp.int32)
    matches = indices[:, None] == positions[None, :]
    return jnp.sum(jnp.where(matches, entries[None, :], 0.0), axis=1)


def scatter_shards(factors, partner, occupied_energy, partner_energy, virtual_energy):
    aux_rows, local_occ, virt_count = factors.shape
    partner_full = lax.all_gather(partner, "occ", axis=1, tiled=True)
    flat_factors = factors.reshape(aux_rows, local_occ * virt_count)
    total_rows = local_occ * virt_count
    row_share = total_rows // lax.axis_size("aux")
    own_first = lax.axis_index("aux") * row_share
    integrals = lax.psum_scatter(
        lax.dot_general(flat_factors, partner_full, (((0,), (0,)), ((), ())), preferred_element_type=F32).astype(BF16),
        "aux",
        scatter_dimension=0,
        tiled=True,
    ).astype(F32)
    row_ids = own_first + jnp.arange(row_share, dtype=jnp.int32)
    occ_part = lookup(occupied_energy, row_ids // virt_count)
    virt_part = lookup(virtual_energy, row_ids % virt_count)
    divisor = virt_part[:, None] + virtual_energy[None, :] - occ_part[:, None] - partner_energy[0]
    amp_shard = (-integrals / divisor).astype(BF16)
    amp_full = lax.all_gather(amp_shard, "aux", axis=0, tiled=True)
    amp_cube = amp_full.reshape(local_occ, virt_count, virt_count)
    direct = jnp.einsum("qb,iab->qia", partner_full, amp_cube, preferred_element_type=F32)
    swapped = jnp.einsum("qb,iba->qia", partner_full, amp_cube, preferred_element_type=F32)
    density = (2.0 * direct - swapped).astype(BF16)
    return (amp_shard, density)


MIB = 1024 * 1024


WHOLE = pl.BlockSpec(memory_space=pltpu.VMEM)
UNREAD = pl.BlockSpec(memory_space=pl.ANY)
LANES = 128


def kernel(body, name, mib, out, inputs, unread=(), scratch=(), grid=None, out_specs=None):
    count = len(inputs)

    def without_unread(*refs):
        body(*refs[:count], *refs[count + len(unread) :])

    return pl.pallas_call(
        without_unread,
        grid=grid or (),
        in_specs=[WHOLE] * count + [UNREAD] * len(unread),
        out_specs=out_specs or jax.tree.map(lambda _: WHOLE, out),
        out_shape=out,
        scratch_shapes=list(scratch),
        compiler_params=pltpu.CompilerParams(vmem_limit_bytes=mib * 1024 * 1024),
        cost_estimate=pl.CostEstimate(flops=1, bytes_accessed=1, transcendentals=0),
        name=name,
    )(*inputs, *unread)


def shaped(shape, dtype=BF16):
    return jax.ShapeDtypeStruct(shape, dtype)


def turn(near_shard, far_shard, occupied_energy, partner_energy, virtual_energy, *unread):
    aux_rows, width = near_shard.shape
    virt_count = virtual_energy.shape[1]

    def body(a_ref, b_ref, occupied_ref, partner_ref, virtual_ref, out_ref, rows_ref, columns_ref):
        out_ref[0] = a_ref[...].T
        out_ref[1] = b_ref[...].T
        rows_ref[...] = jnp.broadcast_to(virtual_ref[...], (LANES, virt_count)).T
        first, second = occupied_ref[:, 0:1], occupied_ref[:, 1:2]
        near = near_place() == 1
        virtual = virtual_ref[...] - partner_ref[...]
        columns_ref[:, :virt_count] = virtual - jnp.where(near, second, first)
        columns_ref[:, virt_count:] = virtual - jnp.where(near, first, second)

    out = [shaped((2, width, aux_rows)), shaped((virt_count, LANES), F32), shaped((1, 2 * virt_count), F32)]
    inputs = (near_shard, far_shard, occupied_energy, partner_energy, virtual_energy)
    return kernel(body, "turn_shards", 8, out, inputs, unread)


def pick(flat, spans, *unread):
    aux_rows, width = flat.shape
    unit = width // 8

    def body(flat_ref, *out_refs):
        shift = jnp.where(near_place() == 1, 0, width // 2)
        for (first, last), out_ref in zip(spans, out_refs, strict=True):
            for at in range(first, last, unit):
                source = lax.rem(at + shift, width)
                out_ref[:, at - first : at - first + unit] = flat_ref[:, pl.ds(pl.multiple_of(source, unit), unit)]

    return kernel(body, "pick_pieces", 8, [shaped((aux_rows, b - a)) for a, b in spans], (flat,), unread)


def held(block, *unread):
    def body(block_ref, out_ref):
        out_ref[...] = block_ref[...]

    return kernel(body, "held_block", 8, shaped(block.shape), (block,), unread)


def assemble(blocks):
    _, width, aux_rows = blocks[0].shape
    virt_count = width * len(blocks)

    def body(*refs):
        own_t_ref, far_t_ref, own_ref = refs[-3:]
        for k, ref in enumerate(refs[:-3]):
            first = pl.multiple_of((lax.axis_index("occ") ^ k) * width, width)
            own_t_ref[pl.ds(first, width), :] = ref[0]
            far_t_ref[pl.ds(first, width), :] = ref[1]
            own_ref[:, pl.ds(first, width)] = ref[0].T

    out = [shaped((virt_count, aux_rows))] * 2 + [shaped((aux_rows, virt_count))]
    return kernel(body, "assemble_partner", 12, out, tuple(blocks))


def near_place():
    return lax.axis_index("aux") // 2


def core_place():
    return lax.axis_index("aux") % 2


def dot_rows(own, amp):
    return jnp.dot(own, amp, preferred_element_type=F32)


def dot_columns(own, amp):
    return lax.dot_general(own, amp, (((1,), (1,)), ((), ())), preferred_element_type=F32)


def partial_integrals(own_t, far_t, flat, fetched, first, *unread):
    virt_count = own_t.shape[0]
    width, share = flat.shape[1], fetched.shape[1]
    unit = width // 8

    def body(own_ref, far_ref, flat_ref, fetched_ref, *out_refs):
        shift = jnp.where(near_place() == 1, width // 2, 0)
        for n, out_ref in enumerate(out_refs):
            source = pl.multiple_of(lax.rem(first + n * unit + shift, width), unit)
            total = dot_rows(own_ref[...], flat_ref[:, pl.ds(source, unit)])
            total += dot_rows(far_ref[...], fetched_ref[:, n * unit : (n + 1) * unit])
            out_ref[...] = total.astype(BF16)

    out = [shaped((virt_count, unit))] * (share // unit)
    return kernel(body, "partial_integrals", 12, out, (own_t, far_t, flat, fetched), unread)


def amplitude_bands(rows_ref, columns_ref, first, part_refs, other_refs, out_ref):
    virt_count, unit = part_refs[0].shape
    block = 32

    for n, (part_ref, other_ref) in enumerate(zip(part_refs, other_refs, strict=True)):
        at = slice(n * unit, (n + 1) * unit)
        column = jnp.broadcast_to(columns_ref[:, first + n * unit : first + (n + 1) * unit], (8, unit))

        @pl.loop(0, virt_count // block, unroll=2)
        def _(r, at=at, column=column, part_ref=part_ref, other_ref=other_ref):
            band = pl.ds(pl.multiple_of(r * block, block), block)
            divisor = jnp.concatenate([rows_ref[band, :]] * (unit // LANES), axis=1)
            divisor = divisor + jnp.concatenate([column] * (block // 8), axis=0)
            integrals = part_ref[band, :].astype(F32) + other_ref[band, :].astype(F32)
            inverse = pl.reciprocal(divisor, approx=True)
            inverse = inverse * (divisor * inverse - 2.0)
            out_ref[band, at] = (integrals * inverse).astype(BF16)


def amplitude_piece(rows, columns, first, parts, others, *unread):
    count = len(parts)
    virt_count, unit = parts[0].shape

    def body(rows_ref, columns_ref, *refs):
        amplitude_bands(rows_ref, columns_ref, first, refs[:count], refs[count:-1], refs[-1])

    out = shaped((virt_count, count * unit))
    return kernel(body, "amplitude_piece", 12, out, (rows, columns, *parts, *others), unread)


def clip_spans(spans, low, high):
    found = []
    for n, (first, last) in enumerate(spans):
        a, b = max(first, low), min(last, high)
        if a < b:
            found.append((n, a - first, a - low, b - low))
    return found


def own_amplitudes(amps, spans, virt_count, *unread):
    half, unit = virt_count // 2, virt_count // 4

    def body(*refs):
        for core in range(2):

            @pl.when(core_place() == core)
            def _():
                for n, skip, a, b in clip_spans(spans, core * half, (core + 1) * half):
                    for r in range(0, virt_count, unit):
                        refs[-1][a:b, r : r + unit] = refs[n][r : r + unit, skip : skip + b - a].T

    return kernel(body, "own_amplitudes", 12, shaped((half, virt_count)), tuple(amps), unread)


def add_terms(total, own_ref, amp_refs, found, at, unit):
    for n, skip, a, b in found:
        total = total - dot_columns(own_ref[:, a:b], amp_refs[n][at : at + unit, skip : skip + b - a])
    for n, skip, a, b in found:
        if a <= at < b:
            rows = own_ref[...]
            total = total + dot_rows(rows + rows, amp_refs[n][:, skip + at - a : skip + at - a + unit])
    return total


def density_terms(own, amps, found, dtype, *unread):
    aux_rows, virt_count = own.shape
    unit = virt_count // 4

    def body(own_ref, *refs):
        for at in range(0, virt_count, unit):
            total = add_terms(jnp.zeros((aux_rows, unit), F32), own_ref, refs[:-1], found, at, unit)
            refs[-1][:, at : at + unit] = total.astype(dtype)

    return kernel(body, "density_terms", 16, shaped((aux_rows, virt_count), dtype), (own, *amps), unread)


def finish(rows, columns, first, parts, others, own, earlier, near_density):
    count = len(parts)
    virt_count, unit = parts[0].shape
    aux_rows, share = own.shape[0], count * unit
    block = aux_rows // 2
    found = [(0, 0, virt_count - share, virt_count)]

    def body(rows_ref, columns_ref, *refs):
        part_refs, other_refs = refs[:count], refs[count : 2 * count]
        own_ref, earlier_ref, ready_ref, out_ref, amp_ref, density_ref = refs[2 * count :]
        step = pl.program_id(0)

        @pl.when(step == 0)
        def _():
            amplitude_bands(rows_ref, columns_ref, first, part_refs, other_refs, amp_ref)
            for at in range(0, virt_count, unit):
                total = add_terms(earlier_ref[:, at : at + unit], own_ref, [amp_ref], found, at, unit)
                density_ref[:, at : at + unit] = total.astype(BF16)

        band = pl.ds(pl.multiple_of(step * block, block), block)
        density, ready = density_ref[band, :], ready_ref[band, :]
        swap = near_place() == 1
        out_ref[:, 0, :] = jnp.where(swap, density, ready)
        out_ref[:, 1, :] = jnp.where(swap, ready, density)

    return kernel(
        body,
        "finish_density",
        20,
        shaped((aux_rows, 2, virt_count)),
        (rows, columns, *parts, *others, own, earlier, near_density),
        scratch=[pltpu.VMEM((virt_count, share), BF16), pltpu.VMEM((aux_rows, virt_count), BF16)],
        grid=(aux_rows // block,),
        out_specs=pl.BlockSpec((block, 2, virt_count), lambda n: (n, 0, 0)),
    )


def pair_shards(factors, partner, occupied_energy, partner_energy, virtual_energy):
    aux_rows, local_occ, virt_count = factors.shape
    n_aux = lax.axis_size("aux")
    n_occ = lax.axis_size("occ")
    width, unit = local_occ * virt_count, virt_count // 4
    across = [(d, (d + n_aux // 2) % n_aux) for d in range(n_aux)]
    within = [(d, d ^ 1) for d in range(n_aux)]
    def occ_swap(value, k):
        return lax.ppermute(value, "occ", [(d, d ^ k) for d in range(n_occ)])

    far = lax.ppermute(partner, "aux", across)
    flat = factors.reshape(aux_rows, width)
    edges = [n * unit for n in (0, 1, 3, 7, 8)]
    spans = list(zip(edges[:-1], edges[1:], strict=True))
    last = len(spans) - 1
    sent = pick(flat, spans[:1])
    sent += pick(flat, spans[1:], sent[0])
    fetched = [lax.ppermute(piece, "aux", across) for piece in sent]

    line = virtual_energy.reshape(1, virt_count)
    occupied, resident = occupied_energy.reshape(1, local_occ), partner_energy.reshape(1, 1)
    shard, rows, columns = turn(partner, far, occupied, resident, line, sent[0])
    by_4 = occ_swap(shard, 4)
    by_2 = occ_swap(shard, 2)
    by_1 = occ_swap(shard, 1)
    by_3 = occ_swap(held(by_2, by_1, fetched[0]), 1)
    by_4 = held(by_4, fetched[1])
    by_7 = occ_swap(by_3, 4)
    by_6 = occ_swap(by_4, 2)
    by_5 = occ_swap(by_4, 1)
    own_t, far_t, own = assemble([shard, by_1, by_2, by_3, by_4, by_5, by_6, by_7])

    def partial(n, *unread):
        return partial_integrals(own_t, far_t, flat, fetched[n], spans[n][0], *unread)

    def other_core(parts):
        return [lax.ppermute(part, "aux", within) for part in parts]

    def amplitudes(n, part, *unread):
        return amplitude_piece(rows, columns, n * unit, [part], other_core([part]), *unread)

    eighths = [(n * unit, (n + 1) * unit) for n in range(8)]
    parts = partial(0)
    parts += partial(1, parts[0])
    amps = [amplitudes(n, part) for n, part in enumerate(parts)]
    parts = partial(2, *amps)
    amps.append(amplitudes(3, parts[0]))
    near_density = density_terms(own, amps, clip_spans(eighths[:4], 0, virt_count), BF16)
    more = [amplitudes(n, part, near_density) for n, part in enumerate(parts[1:], 4)]
    earlier = density_terms(own, more, clip_spans(eighths[4:7], virt_count, width), F32)
    parts = partial(last, earlier)
    others = other_core(parts)
    amp_shard = own_amplitudes(amps, eighths[:4], virt_count, parts[0])
    density = finish(rows, columns, spans[last][0], parts, others, own, earlier, near_density)
    return (amp_shard, density)


def solution(mesh):
    n_aux, n_occ = mesh.shape["aux"], mesh.shape["occ"]
    fetch = n_aux == 2 * 2 and n_occ == 2 * 2 * 2
    return jax.shard_map(
        pair_shards if fetch else scatter_shards,
        mesh=mesh,
        in_specs=(P("aux", "occ", None), P("aux", "occ"), P("occ"), P(), P()),
        out_specs=(P(("occ", "aux"), None), P("aux", "occ", None)),
        check_vma=False,
    )
```

```python
import jax
import jax.numpy as jnp
from jax import lax
from jax.experimental import pallas as pl
from jax.experimental.pallas import tpu as pltpu
from jax.sharding import PartitionSpec as P

BF16 = jnp.bfloat16
F32 = jnp.float32


def lookup(entries, indices):
    positions = jnp.arange(entries.shape[0], dtype=jnp.int32)
    matches = indices[:, None] == positions[None, :]
    return jnp.sum(jnp.where(matches, entries[None, :], 0.0), axis=1)


def scatter_shards(factors, partner, occupied_energy, partner_energy, virtual_energy):
    aux_rows, local_occ, virt_count = factors.shape
    partner_full = lax.all_gather(partner, "occ", axis=1, tiled=True)
    flat_factors = factors.reshape(aux_rows, local_occ * virt_count)
    total_rows = local_occ * virt_count
    row_share = total_rows // lax.axis_size("aux")
    own_first = lax.axis_index("aux") * row_share
    integrals = lax.psum_scatter(
        lax.dot_general(flat_factors, partner_full, (((0,), (0,)), ((), ())), preferred_element_type=F32).astype(BF16),
        "aux",
        scatter_dimension=0,
        tiled=True,
    ).astype(F32)
    row_ids = own_first + jnp.arange(row_share, dtype=jnp.int32)
    occ_part = lookup(occupied_energy, row_ids // virt_count)
    virt_part = lookup(virtual_energy, row_ids % virt_count)
    divisor = virt_part[:, None] + virtual_energy[None, :] - occ_part[:, None] - partner_energy[0]
    amp_shard = (-integrals / divisor).astype(BF16)
    amp_full = lax.all_gather(amp_shard, "aux", axis=0, tiled=True)
    amp_cube = amp_full.reshape(local_occ, virt_count, virt_count)
    direct = jnp.einsum("qb,iab->qia", partner_full, amp_cube, preferred_element_type=F32)
    swapped = jnp.einsum("qb,iba->qia", partner_full, amp_cube, preferred_element_type=F32)
    density = (2.0 * direct - swapped).astype(BF16)
    return (amp_shard, density)


MIB = 1024 * 1024


WHOLE = pl.BlockSpec(memory_space=pltpu.VMEM)
UNREAD = pl.BlockSpec(memory_space=pl.ANY)
LANES = 128


def kernel(body, name, mib, out, inputs, unread=(), scratch=(), grid=None, out_specs=None):
    count = len(inputs)

    def without_unread(*refs):
        body(*refs[:count], *refs[count + len(unread) :])

    return pl.pallas_call(
        without_unread,
        grid=grid or (),
        in_specs=[WHOLE] * count + [UNREAD] * len(unread),
        out_specs=out_specs or jax.tree.map(lambda _: WHOLE, out),
        out_shape=out,
        scratch_shapes=list(scratch),
        compiler_params=pltpu.CompilerParams(vmem_limit_bytes=mib * 1024 * 1024),
        cost_estimate=pl.CostEstimate(flops=1, bytes_accessed=1, transcendentals=0),
        name=name,
    )(*inputs, *unread)


def shaped(shape, dtype=BF16):
    return jax.ShapeDtypeStruct(shape, dtype)


def turn(near_shard, far_shard, occupied_energy, partner_energy, virtual_energy, *unread):
    aux_rows, width = near_shard.shape
    virt_count = virtual_energy.shape[1]

    def body(a_ref, b_ref, occupied_ref, partner_ref, virtual_ref, out_ref, rows_ref, columns_ref):
        out_ref[0] = a_ref[...].T
        out_ref[1] = b_ref[...].T
        rows_ref[...] = jnp.broadcast_to(virtual_ref[...], (LANES, virt_count)).T
        first, second = occupied_ref[:, 0:1], occupied_ref[:, 1:2]
        near = near_place() == 1
        virtual = virtual_ref[...] - partner_ref[...]
        columns_ref[:, :virt_count] = virtual - jnp.where(near, second, first)
        columns_ref[:, virt_count:] = virtual - jnp.where(near, first, second)

    out = [shaped((2, width, aux_rows)), shaped((virt_count, LANES), F32), shaped((1, 2 * virt_count), F32)]
    inputs = (near_shard, far_shard, occupied_energy, partner_energy, virtual_energy)
    return kernel(body, "turn_shards", 8, out, inputs, unread)


def pick(flat, spans, *unread):
    aux_rows, width = flat.shape
    unit = width // 8

    def body(flat_ref, *out_refs):
        shift = jnp.where(near_place() == 1, 0, width // 2)
        for (first, last), out_ref in zip(spans, out_refs, strict=True):
            for at in range(first, last, unit):
                source = lax.rem(at + shift, width)
                out_ref[:, at - first : at - first + unit] = flat_ref[:, pl.ds(pl.multiple_of(source, unit), unit)]

    return kernel(body, "pick_pieces", 8, [shaped((aux_rows, b - a)) for a, b in spans], (flat,), unread)


def held(block, *unread):
    def body(block_ref, out_ref):
        out_ref[...] = block_ref[...]

    return kernel(body, "held_block", 8, shaped(block.shape), (block,), unread)


def assemble(blocks):
    _, width, aux_rows = blocks[0].shape
    virt_count = width * len(blocks)

    def body(*refs):
        own_t_ref, far_t_ref, own_ref = refs[-3:]
        for k, ref in enumerate(refs[:-3]):
            first = pl.multiple_of((lax.axis_index("occ") ^ k) * width, width)
            own_t_ref[pl.ds(first, width), :] = ref[0]
            far_t_ref[pl.ds(first, width), :] = ref[1]
            own_ref[:, pl.ds(first, width)] = ref[0].T

    out = [shaped((virt_count, aux_rows))] * 2 + [shaped((aux_rows, virt_count))]
    return kernel(body, "assemble_partner", 12, out, tuple(blocks))


def near_place():
    return lax.axis_index("aux") // 2


def core_place():
    return lax.axis_index("aux") % 2


def dot_rows(own, amp):
    return jnp.dot(own, amp, preferred_element_type=F32)


def dot_columns(own, amp):
    return lax.dot_general(own, amp, (((1,), (1,)), ((), ())), preferred_element_type=F32)


def partial_integrals(own_t, far_t, flat, fetched, first, *unread):
    virt_count = own_t.shape[0]
    width, share = flat.shape[1], fetched.shape[1]
    unit = width // 8

    def body(own_ref, far_ref, flat_ref, fetched_ref, *out_refs):
        shift = jnp.where(near_place() == 1, width // 2, 0)
        for n, out_ref in enumerate(out_refs):
            source = pl.multiple_of(lax.rem(first + n * unit + shift, width), unit)
            total = dot_rows(own_ref[...], flat_ref[:, pl.ds(source, unit)])
            total += dot_rows(far_ref[...], fetched_ref[:, n * unit : (n + 1) * unit])
            out_ref[...] = total.astype(BF16)

    out = [shaped((virt_count, unit))] * (share // unit)
    return kernel(body, "partial_integrals", 12, out, (own_t, far_t, flat, fetched), unread)


def amplitude_bands(rows_ref, columns_ref, first, part_refs, other_refs, out_ref):
    virt_count, unit = part_refs[0].shape
    block = 32

    for n, (part_ref, other_ref) in enumerate(zip(part_refs, other_refs, strict=True)):
        at = slice(n * unit, (n + 1) * unit)
        column = jnp.broadcast_to(columns_ref[:, first + n * unit : first + (n + 1) * unit], (8, unit))

        @pl.loop(0, virt_count // block, unroll=2)
        def _(r, at=at, column=column, part_ref=part_ref, other_ref=other_ref):
            band = pl.ds(pl.multiple_of(r * block, block), block)
            divisor = jnp.concatenate([rows_ref[band, :]] * (unit // LANES), axis=1)
            divisor = divisor + jnp.concatenate([column] * (block // 8), axis=0)
            integrals = part_ref[band, :].astype(F32) + other_ref[band, :].astype(F32)
            inverse = pl.reciprocal(divisor, approx=True)
            inverse = inverse * (divisor * inverse - 2.0)
            out_ref[band, at] = (integrals * inverse).astype(BF16)


def amplitude_piece(rows, columns, first, parts, others, *unread):
    count = len(parts)
    virt_count, unit = parts[0].shape

    def body(rows_ref, columns_ref, *refs):
        amplitude_bands(rows_ref, columns_ref, first, refs[:count], refs[count:-1], refs[-1])

    out = shaped((virt_count, count * unit))
    return kernel(body, "amplitude_piece", 12, out, (rows, columns, *parts, *others), unread)


def clip_spans(spans, low, high):
    found = []
    for n, (first, last) in enumerate(spans):
        a, b = max(first, low), min(last, high)
        if a < b:
            found.append((n, a - first, a - low, b - low))
    return found


def own_amplitudes(amps, spans, virt_count, *unread):
    half, unit = virt_count // 2, virt_count // 4

    def body(*refs):
        for core in range(2):

            @pl.when(core_place() == core)
            def _():
                for n, skip, a, b in clip_spans(spans, core * half, (core + 1) * half):
                    for r in range(0, virt_count, unit):
                        refs[-1][a:b, r : r + unit] = refs[n][r : r + unit, skip : skip + b - a].T

    return kernel(body, "own_amplitudes", 12, shaped((half, virt_count)), tuple(amps), unread)


def add_terms(total, own_ref, amp_refs, found, at, unit):
    for n, skip, a, b in found:
        total = total - dot_columns(own_ref[:, a:b], amp_refs[n][at : at + unit, skip : skip + b - a])
    for n, skip, a, b in found:
        if a <= at < b:
            rows = own_ref[...]
            total = total + dot_rows(rows + rows, amp_refs[n][:, skip + at - a : skip + at - a + unit])
    return total


def density_terms(own, amps, found, dtype, *unread):
    aux_rows, virt_count = own.shape
    unit = virt_count // 4

    def body(own_ref, *refs):
        for at in range(0, virt_count, unit):
            total = add_terms(jnp.zeros((aux_rows, unit), F32), own_ref, refs[:-1], found, at, unit)
            refs[-1][:, at : at + unit] = total.astype(dtype)

    return kernel(body, "density_terms", 16, shaped((aux_rows, virt_count), dtype), (own, *amps), unread)


def finish(rows, columns, first, parts, others, own, earlier, near_density):
    count = len(parts)
    virt_count, unit = parts[0].shape
    aux_rows, share = own.shape[0], count * unit
    block = aux_rows // 2
    found = [(0, 0, virt_count - share, virt_count)]

    def body(rows_ref, columns_ref, *refs):
        part_refs, other_refs = refs[:count], refs[count : 2 * count]
        own_ref, earlier_ref, ready_ref, out_ref, amp_ref, density_ref = refs[2 * count :]
        step = pl.program_id(0)

        @pl.when(step == 0)
        def _():
            amplitude_bands(rows_ref, columns_ref, first, part_refs, other_refs, amp_ref)
            for at in range(0, virt_count, unit):
                total = add_terms(earlier_ref[:, at : at + unit], own_ref, [amp_ref], found, at, unit)
                density_ref[:, at : at + unit] = total.astype(BF16)

        band = pl.ds(pl.multiple_of(step * block, block), block)
        density, ready = density_ref[band, :], ready_ref[band, :]
        swap = near_place() == 1
        out_ref[:, 0, :] = jnp.where(swap, density, ready)
        out_ref[:, 1, :] = jnp.where(swap, ready, density)

    return kernel(
        body,
        "finish_density",
        20,
        shaped((aux_rows, 2, virt_count)),
        (rows, columns, *parts, *others, own, earlier, near_density),
        scratch=[pltpu.VMEM((virt_count, share), BF16), pltpu.VMEM((aux_rows, virt_count), BF16)],
        grid=(aux_rows // block,),
        out_specs=pl.BlockSpec((block, 2, virt_count), lambda n: (n, 0, 0)),
    )


def pair_shards(factors, partner, occupied_energy, partner_energy, virtual_energy):
    aux_rows, local_occ, virt_count = factors.shape
    n_aux = lax.axis_size("aux")
    n_occ = lax.axis_size("occ")
    width, unit = local_occ * virt_count, virt_count // 4
    across = [(d, (d + n_aux // 2) % n_aux) for d in range(n_aux)]
    within = [(d, d ^ 1) for d in range(n_aux)]
    def occ_swap(value, k):
        return lax.ppermute(value, "occ", [(d, d ^ k) for d in range(n_occ)])

    far = lax.ppermute(partner, "aux", across)
    flat = factors.reshape(aux_rows, width)
    edges = [n * unit for n in (0, 1, 3, 7, 8)]
    spans = list(zip(edges[:-1], edges[1:], strict=True))
    last = len(spans) - 1
    sent = pick(flat, spans[:1])
    sent += pick(flat, spans[1:], sent[0])
    fetched = [lax.ppermute(piece, "aux", across) for piece in sent]

    line = virtual_energy.reshape(1, virt_count)
    occupied, resident = occupied_energy.reshape(1, local_occ), partner_energy.reshape(1, 1)
    shard, rows, columns = turn(partner, far, occupied, resident, line, sent[0])
    by_4 = occ_swap(held(shard, fetched[0]), 4)
    by_2 = occ_swap(shard, 2)
    by_1 = occ_swap(shard, 1)
    by_3 = occ_swap(held(by_2, by_1, fetched[0]), 1)
    by_4 = held(by_4, fetched[1])
    by_7 = occ_swap(by_3, 4)
    by_6 = occ_swap(by_4, 2)
    by_5 = occ_swap(by_4, 1)
    own_t, far_t, own = assemble([shard, by_1, by_2, by_3, by_4, by_5, by_6, by_7])

    def partial(n, *unread):
        return partial_integrals(own_t, far_t, flat, fetched[n], spans[n][0], *unread)

    def other_core(parts):
        return [lax.ppermute(part, "aux", within) for part in parts]

    def amplitudes(n, part, *unread):
        return amplitude_piece(rows, columns, n * unit, [part], other_core([part]), *unread)

    eighths = [(n * unit, (n + 1) * unit) for n in range(8)]
    parts = partial(0)
    parts += partial(1, parts[0])
    amps = [amplitudes(n, part) for n, part in enumerate(parts)]
    parts = partial(2, *amps)
    amps.append(amplitudes(3, parts[0]))
    near_density = density_terms(own, amps, clip_spans(eighths[:4], 0, virt_count), BF16)
    more = [amplitudes(n, part, near_density) for n, part in enumerate(parts[1:], 4)]
    earlier = density_terms(own, more, clip_spans(eighths[4:7], virt_count, width), F32)
    parts = partial(last, earlier)
    others = other_core(parts)
    amp_shard = own_amplitudes(amps, eighths[:4], virt_count, parts[0])
    density = finish(rows, columns, spans[last][0], parts, others, own, earlier, near_density)
    return (amp_shard, density)


def solution(mesh):
    n_aux, n_occ = mesh.shape["aux"], mesh.shape["occ"]
    fetch = n_aux == 2 * 2 and n_occ == 2 * 2 * 2
    return jax.shard_map(
        pair_shards if fetch else scatter_shards,
        mesh=mesh,
        in_specs=(P("aux", "occ", None), P("aux", "occ"), P("occ"), P(), P()),
        out_specs=(P(("occ", "aux"), None), P("aux", "occ", None)),
        check_vma=False,
    )
```

```python
import jax
import jax.numpy as jnp
from jax import lax
from jax.experimental import pallas as pl
from jax.experimental.pallas import tpu as pltpu
from jax.sharding import PartitionSpec as P

BF16 = jnp.bfloat16
F32 = jnp.float32


def lookup(entries, indices):
    positions = jnp.arange(entries.shape[0], dtype=jnp.int32)
    matches = indices[:, None] == positions[None, :]
    return jnp.sum(jnp.where(matches, entries[None, :], 0.0), axis=1)


def scatter_shards(factors, partner, occupied_energy, partner_energy, virtual_energy):
    aux_rows, local_occ, virt_count = factors.shape
    partner_full = lax.all_gather(partner, "occ", axis=1, tiled=True)
    flat_factors = factors.reshape(aux_rows, local_occ * virt_count)
    total_rows = local_occ * virt_count
    row_share = total_rows // lax.axis_size("aux")
    own_first = lax.axis_index("aux") * row_share
    integrals = lax.psum_scatter(
        lax.dot_general(flat_factors, partner_full, (((0,), (0,)), ((), ())), preferred_element_type=F32).astype(BF16),
        "aux",
        scatter_dimension=0,
        tiled=True,
    ).astype(F32)
    row_ids = own_first + jnp.arange(row_share, dtype=jnp.int32)
    occ_part = lookup(occupied_energy, row_ids // virt_count)
    virt_part = lookup(virtual_energy, row_ids % virt_count)
    divisor = virt_part[:, None] + virtual_energy[None, :] - occ_part[:, None] - partner_energy[0]
    amp_shard = (-integrals / divisor).astype(BF16)
    amp_full = lax.all_gather(amp_shard, "aux", axis=0, tiled=True)
    amp_cube = amp_full.reshape(local_occ, virt_count, virt_count)
    direct = jnp.einsum("qb,iab->qia", partner_full, amp_cube, preferred_element_type=F32)
    swapped = jnp.einsum("qb,iba->qia", partner_full, amp_cube, preferred_element_type=F32)
    density = (2.0 * direct - swapped).astype(BF16)
    return (amp_shard, density)


MIB = 1024 * 1024


WHOLE = pl.BlockSpec(memory_space=pltpu.VMEM)
UNREAD = pl.BlockSpec(memory_space=pl.ANY)
LANES = 128


def kernel(body, name, mib, out, inputs, unread=(), scratch=(), grid=None, out_specs=None):
    count = len(inputs)

    def without_unread(*refs):
        body(*refs[:count], *refs[count + len(unread) :])

    return pl.pallas_call(
        without_unread,
        grid=grid or (),
        in_specs=[WHOLE] * count + [UNREAD] * len(unread),
        out_specs=out_specs or jax.tree.map(lambda _: WHOLE, out),
        out_shape=out,
        scratch_shapes=list(scratch),
        compiler_params=pltpu.CompilerParams(vmem_limit_bytes=mib * 1024 * 1024),
        cost_estimate=pl.CostEstimate(flops=1, bytes_accessed=1, transcendentals=0),
        name=name,
    )(*inputs, *unread)


def shaped(shape, dtype=BF16):
    return jax.ShapeDtypeStruct(shape, dtype)


def turn(near_shard, far_shard, occupied_energy, partner_energy, virtual_energy, *unread):
    aux_rows, width = near_shard.shape
    virt_count = virtual_energy.shape[1]

    def body(a_ref, b_ref, occupied_ref, partner_ref, virtual_ref, out_ref, rows_ref, columns_ref):
        out_ref[0] = a_ref[...].T
        out_ref[1] = b_ref[...].T
        rows_ref[...] = jnp.broadcast_to(virtual_ref[...], (LANES, virt_count)).T
        first, second = occupied_ref[:, 0:1], occupied_ref[:, 1:2]
        near = near_place() == 1
        virtual = virtual_ref[...] - partner_ref[...]
        columns_ref[:, :virt_count] = virtual - jnp.where(near, second, first)
        columns_ref[:, virt_count:] = virtual - jnp.where(near, first, second)

    out = [shaped((2, width, aux_rows)), shaped((virt_count, LANES), F32), shaped((1, 2 * virt_count), F32)]
    inputs = (near_shard, far_shard, occupied_energy, partner_energy, virtual_energy)
    return kernel(body, "turn_shards", 8, out, inputs, unread)


def pick(flat, spans, *unread):
    aux_rows, width = flat.shape
    unit = min(last - first for first, last in spans)

    def body(flat_ref, *out_refs):
        shift = jnp.where(near_place() == 1, 0, width // 2)
        for (first, last), out_ref in zip(spans, out_refs, strict=True):
            for at in range(first, last, unit):
                source = lax.rem(at + shift, width)
                out_ref[:, at - first : at - first + unit] = flat_ref[:, pl.ds(pl.multiple_of(source, unit), unit)]

    return kernel(body, "pick_pieces", 8, [shaped((aux_rows, b - a)) for a, b in spans], (flat,), unread)


def held(block, *unread):
    def body(block_ref, out_ref):
        out_ref[...] = block_ref[...]

    return kernel(body, "held_block", 8, shaped(block.shape), (block,), unread)


def assemble(blocks):
    _, width, aux_rows = blocks[0].shape
    virt_count = width * len(blocks)

    def body(*refs):
        own_t_ref, far_t_ref, own_ref = refs[-3:]
        for k, ref in enumerate(refs[:-3]):
            first = pl.multiple_of((lax.axis_index("occ") ^ k) * width, width)
            own_t_ref[pl.ds(first, width), :] = ref[0]
            far_t_ref[pl.ds(first, width), :] = ref[1]
            own_ref[:, pl.ds(first, width)] = ref[0].T

    out = [shaped((virt_count, aux_rows))] * 2 + [shaped((aux_rows, virt_count))]
    return kernel(body, "assemble_partner", 12, out, tuple(blocks))


def near_place():
    return lax.axis_index("aux") // 2


def core_place():
    return lax.axis_index("aux") % 2


def dot_rows(own, amp):
    return jnp.dot(own, amp, preferred_element_type=F32)


def dot_columns(own, amp):
    return lax.dot_general(own, amp, (((1,), (1,)), ((), ())), preferred_element_type=F32)


def partial_integrals(own_t, far_t, flat, fetched, first, *unread):
    virt_count = own_t.shape[0]
    width, share = flat.shape[1], fetched.shape[1]
    unit = width // 8

    def body(own_ref, far_ref, flat_ref, fetched_ref, *out_refs):
        shift = jnp.where(near_place() == 1, width // 2, 0)
        for n, out_ref in enumerate(out_refs):
            source = pl.multiple_of(lax.rem(first + n * unit + shift, width), unit)
            total = dot_rows(own_ref[...], flat_ref[:, pl.ds(source, unit)])
            total += dot_rows(far_ref[...], fetched_ref[:, n * unit : (n + 1) * unit])
            out_ref[...] = total.astype(BF16)

    out = [shaped((virt_count, unit))] * (share // unit)
    return kernel(body, "partial_integrals", 12, out, (own_t, far_t, flat, fetched), unread)


def amplitude_bands(rows_ref, columns_ref, first, part_refs, other_refs, out_ref):
    virt_count, unit = part_refs[0].shape
    block = 32

    for n, (part_ref, other_ref) in enumerate(zip(part_refs, other_refs, strict=True)):
        at = slice(n * unit, (n + 1) * unit)
        column = jnp.broadcast_to(columns_ref[:, first + n * unit : first + (n + 1) * unit], (8, unit))

        @pl.loop(0, virt_count // block, unroll=2)
        def _(r, at=at, column=column, part_ref=part_ref, other_ref=other_ref):
            band = pl.ds(pl.multiple_of(r * block, block), block)
            divisor = jnp.concatenate([rows_ref[band, :]] * (unit // LANES), axis=1)
            divisor = divisor + jnp.concatenate([column] * (block // 8), axis=0)
            integrals = part_ref[band, :].astype(F32) + other_ref[band, :].astype(F32)
            inverse = pl.reciprocal(divisor, approx=True)
            inverse = inverse * (divisor * inverse - 2.0)
            out_ref[band, at] = (integrals * inverse).astype(BF16)


def amplitude_piece(rows, columns, first, parts, others, *unread):
    count = len(parts)
    virt_count, unit = parts[0].shape

    def body(rows_ref, columns_ref, *refs):
        amplitude_bands(rows_ref, columns_ref, first, refs[:count], refs[count:-1], refs[-1])

    out = shaped((virt_count, count * unit))
    return kernel(body, "amplitude_piece", 12, out, (rows, columns, *parts, *others), unread)


def clip_spans(spans, low, high):
    found = []
    for n, (first, last) in enumerate(spans):
        a, b = max(first, low), min(last, high)
        if a < b:
            found.append((n, a - first, a - low, b - low))
    return found


def own_amplitudes(amps, spans, virt_count, *unread):
    half, unit = virt_count // 2, virt_count // 4

    def body(*refs):
        for core in range(2):

            @pl.when(core_place() == core)
            def _():
                for n, skip, a, b in clip_spans(spans, core * half, (core + 1) * half):
                    for r in range(0, virt_count, unit):
                        refs[-1][a:b, r : r + unit] = refs[n][r : r + unit, skip : skip + b - a].T

    return kernel(body, "own_amplitudes", 12, shaped((half, virt_count)), tuple(amps), unread)


def add_terms(total, own_ref, amp_refs, found, at, unit):
    for n, skip, a, b in found:
        total = total - dot_columns(own_ref[:, a:b], amp_refs[n][at : at + unit, skip : skip + b - a])
    for n, skip, a, b in found:
        if a <= at < b:
            rows = own_ref[...]
            total = total + dot_rows(rows + rows, amp_refs[n][:, skip + at - a : skip + at - a + unit])
    return total


def density_terms(own, amps, found, dtype, *unread):
    aux_rows, virt_count = own.shape
    unit = virt_count // 4

    def body(own_ref, *refs):
        for at in range(0, virt_count, unit):
            total = add_terms(jnp.zeros((aux_rows, unit), F32), own_ref, refs[:-1], found, at, unit)
            refs[-1][:, at : at + unit] = total.astype(dtype)

    return kernel(body, "density_terms", 16, shaped((aux_rows, virt_count), dtype), (own, *amps), unread)


def finish(rows, columns, first, parts, others, own, earlier, near_density):
    count = len(parts)
    virt_count, unit = parts[0].shape
    aux_rows, share = own.shape[0], count * unit
    block = aux_rows // 2
    found = [(0, 0, virt_count - share, virt_count)]

    def body(rows_ref, columns_ref, *refs):
        part_refs, other_refs = refs[:count], refs[count : 2 * count]
        own_ref, earlier_ref, ready_ref, out_ref, amp_ref, density_ref = refs[2 * count :]
        step = pl.program_id(0)

        @pl.when(step == 0)
        def _():
            amplitude_bands(rows_ref, columns_ref, first, part_refs, other_refs, amp_ref)
            for at in range(0, virt_count, unit):
                total = add_terms(earlier_ref[:, at : at + unit], own_ref, [amp_ref], found, at, unit)
                density_ref[:, at : at + unit] = total.astype(BF16)

        band = pl.ds(pl.multiple_of(step * block, block), block)
        density, ready = density_ref[band, :], ready_ref[band, :]
        swap = near_place() == 1
        out_ref[:, 0, :] = jnp.where(swap, density, ready)
        out_ref[:, 1, :] = jnp.where(swap, ready, density)

    return kernel(
        body,
        "finish_density",
        20,
        shaped((aux_rows, 2, virt_count)),
        (rows, columns, *parts, *others, own, earlier, near_density),
        scratch=[pltpu.VMEM((virt_count, share), BF16), pltpu.VMEM((aux_rows, virt_count), BF16)],
        grid=(aux_rows // block,),
        out_specs=pl.BlockSpec((block, 2, virt_count), lambda n: (n, 0, 0)),
    )


def pair_shards(factors, partner, occupied_energy, partner_energy, virtual_energy):
    aux_rows, local_occ, virt_count = factors.shape
    n_aux = lax.axis_size("aux")
    n_occ = lax.axis_size("occ")
    width, unit = local_occ * virt_count, virt_count // 4
    across = [(d, (d + n_aux // 2) % n_aux) for d in range(n_aux)]
    within = [(d, d ^ 1) for d in range(n_aux)]
    def occ_swap(value, k):
        return lax.ppermute(value, "occ", [(d, d ^ k) for d in range(n_occ)])

    far = lax.ppermute(partner, "aux", across)
    flat = factors.reshape(aux_rows, width)
    edges = [n * unit for n in (0, 1, 3, 7, 8)]
    spans = list(zip(edges[:-1], edges[1:], strict=True))
    last = len(spans) - 1
    sent = pick(factors[:, :, :unit].reshape(aux_rows, local_occ * unit), spans[:1])

    line = virtual_energy.reshape(1, virt_count)
    occupied, resident = occupied_energy.reshape(1, local_occ), partner_energy.reshape(1, 1)
    shard, rows, columns = turn(partner, far, occupied, resident, line, sent[0])
    sent += pick(flat, spans[1:], sent[0])
    fetched = [lax.ppermute(piece, "aux", across) for piece in sent]
    by_4 = occ_swap(shard, 4)
    by_2 = occ_swap(shard, 2)
    by_1 = occ_swap(shard, 1)
    by_3 = occ_swap(held(by_2, by_1, fetched[0]), 1)
    by_4 = held(by_4, fetched[1])
    by_7 = occ_swap(by_3, 4)
    by_6 = occ_swap(by_4, 2)
    by_5 = occ_swap(by_4, 1)
    own_t, far_t, own = assemble([shard, by_1, by_2, by_3, by_4, by_5, by_6, by_7])

    def partial(n, *unread):
        return partial_integrals(own_t, far_t, flat, fetched[n], spans[n][0], *unread)

    def other_core(parts):
        return [lax.ppermute(part, "aux", within) for part in parts]

    def amplitudes(n, part, *unread):
        return amplitude_piece(rows, columns, n * unit, [part], other_core([part]), *unread)

    eighths = [(n * unit, (n + 1) * unit) for n in range(8)]
    parts = partial(0)
    parts += partial(1, parts[0])
    amps = [amplitudes(n, part) for n, part in enumerate(parts)]
    parts = partial(2, *amps)
    amps.append(amplitudes(3, parts[0]))
    near_density = density_terms(own, amps, clip_spans(eighths[:4], 0, virt_count), BF16)
    more = [amplitudes(n, part, near_density) for n, part in enumerate(parts[1:], 4)]
    earlier = density_terms(own, more, clip_spans(eighths[4:7], virt_count, width), F32)
    parts = partial(last, earlier)
    others = other_core(parts)
    amp_shard = own_amplitudes(amps, eighths[:4], virt_count, parts[0])
    density = finish(rows, columns, spans[last][0], parts, others, own, earlier, near_density)
    return (amp_shard, density)


def solution(mesh):
    n_aux, n_occ = mesh.shape["aux"], mesh.shape["occ"]
    fetch = n_aux == 2 * 2 and n_occ == 2 * 2 * 2
    return jax.shard_map(
        pair_shards if fetch else scatter_shards,
        mesh=mesh,
        in_specs=(P("aux", "occ", None), P("aux", "occ"), P("occ"), P(), P()),
        out_specs=(P(("occ", "aux"), None), P("aux", "occ", None)),
        check_vma=False,
    )
```

```python
import jax
import jax.numpy as jnp
from jax import lax
from jax.experimental import pallas as pl
from jax.experimental.pallas import tpu as pltpu
from jax.sharding import PartitionSpec as P

BF16 = jnp.bfloat16
F32 = jnp.float32


def lookup(entries, indices):
    positions = jnp.arange(entries.shape[0], dtype=jnp.int32)
    matches = indices[:, None] == positions[None, :]
    return jnp.sum(jnp.where(matches, entries[None, :], 0.0), axis=1)


def scatter_shards(factors, partner, occupied_energy, partner_energy, virtual_energy):
    aux_rows, local_occ, virt_count = factors.shape
    partner_full = lax.all_gather(partner, "occ", axis=1, tiled=True)
    flat_factors = factors.reshape(aux_rows, local_occ * virt_count)
    total_rows = local_occ * virt_count
    row_share = total_rows // lax.axis_size("aux")
    own_first = lax.axis_index("aux") * row_share
    integrals = lax.psum_scatter(
        lax.dot_general(flat_factors, partner_full, (((0,), (0,)), ((), ())), preferred_element_type=F32).astype(BF16),
        "aux",
        scatter_dimension=0,
        tiled=True,
    ).astype(F32)
    row_ids = own_first + jnp.arange(row_share, dtype=jnp.int32)
    occ_part = lookup(occupied_energy, row_ids // virt_count)
    virt_part = lookup(virtual_energy, row_ids % virt_count)
    divisor = virt_part[:, None] + virtual_energy[None, :] - occ_part[:, None] - partner_energy[0]
    amp_shard = (-integrals / divisor).astype(BF16)
    amp_full = lax.all_gather(amp_shard, "aux", axis=0, tiled=True)
    amp_cube = amp_full.reshape(local_occ, virt_count, virt_count)
    direct = jnp.einsum("qb,iab->qia", partner_full, amp_cube, preferred_element_type=F32)
    swapped = jnp.einsum("qb,iba->qia", partner_full, amp_cube, preferred_element_type=F32)
    density = (2.0 * direct - swapped).astype(BF16)
    return (amp_shard, density)


MIB = 1024 * 1024


WHOLE = pl.BlockSpec(memory_space=pltpu.VMEM)
UNREAD = pl.BlockSpec(memory_space=pl.ANY)
LANES = 128


def kernel(body, name, mib, out, inputs, unread=(), scratch=(), grid=None, out_specs=None):
    count = len(inputs)

    def without_unread(*refs):
        body(*refs[:count], *refs[count + len(unread) :])

    return pl.pallas_call(
        without_unread,
        grid=grid or (),
        in_specs=[WHOLE] * count + [UNREAD] * len(unread),
        out_specs=out_specs or jax.tree.map(lambda _: WHOLE, out),
        out_shape=out,
        scratch_shapes=list(scratch),
        compiler_params=pltpu.CompilerParams(vmem_limit_bytes=mib * 1024 * 1024),
        cost_estimate=pl.CostEstimate(flops=1, bytes_accessed=1, transcendentals=0),
        name=name,
    )(*inputs, *unread)


def shaped(shape, dtype=BF16):
    return jax.ShapeDtypeStruct(shape, dtype)


def turn(near_shard, far_shard, occupied_energy, partner_energy, virtual_energy, *unread):
    aux_rows, width = near_shard.shape
    virt_count = virtual_energy.shape[1]

    def body(a_ref, b_ref, occupied_ref, partner_ref, virtual_ref, out_ref, rows_ref, columns_ref):
        out_ref[0] = a_ref[...].T
        out_ref[1] = b_ref[...].T
        rows_ref[...] = jnp.broadcast_to(virtual_ref[...], (LANES, virt_count)).T
        first, second = occupied_ref[:, 0:1], occupied_ref[:, 1:2]
        near = near_place() == 1
        virtual = virtual_ref[...] - partner_ref[...]
        columns_ref[:, :virt_count] = virtual - jnp.where(near, second, first)
        columns_ref[:, virt_count:] = virtual - jnp.where(near, first, second)

    out = [shaped((2, width, aux_rows)), shaped((virt_count, LANES), F32), shaped((1, 2 * virt_count), F32)]
    inputs = (near_shard, far_shard, occupied_energy, partner_energy, virtual_energy)
    return kernel(body, "turn_shards", 8, out, inputs, unread)


def pick(flat, spans, *unread):
    aux_rows, width = flat.shape
    unit = min(last - first for first, last in spans)

    def body(flat_ref, *out_refs):
        shift = jnp.where(near_place() == 1, 0, width // 2)
        for (first, last), out_ref in zip(spans, out_refs, strict=True):
            for at in range(first, last, unit):
                source = lax.rem(at + shift, width)
                out_ref[:, at - first : at - first + unit] = flat_ref[:, pl.ds(pl.multiple_of(source, unit), unit)]

    return kernel(body, "pick_pieces", 8, [shaped((aux_rows, b - a)) for a, b in spans], (flat,), unread)


def held(block, *unread):
    def body(block_ref, out_ref):
        out_ref[...] = block_ref[...]

    return kernel(body, "held_block", 8, shaped(block.shape), (block,), unread)


def assemble(blocks):
    _, width, aux_rows = blocks[0].shape
    virt_count = width * len(blocks)

    def body(*refs):
        own_t_ref, far_t_ref, own_ref = refs[-3:]
        for k, ref in enumerate(refs[:-3]):
            first = pl.multiple_of((lax.axis_index("occ") ^ k) * width, width)
            own_t_ref[pl.ds(first, width), :] = ref[0]
            far_t_ref[pl.ds(first, width), :] = ref[1]
            own_ref[:, pl.ds(first, width)] = ref[0].T

    out = [shaped((virt_count, aux_rows))] * 2 + [shaped((aux_rows, virt_count))]
    return kernel(body, "assemble_partner", 12, out, tuple(blocks))


def near_place():
    return lax.axis_index("aux") // 2


def core_place():
    return lax.axis_index("aux") % 2


def dot_rows(own, amp):
    return jnp.dot(own, amp, preferred_element_type=F32)


def dot_columns(own, amp):
    return lax.dot_general(own, amp, (((1,), (1,)), ((), ())), preferred_element_type=F32)


def partial_integrals(own_t, far_t, flat, fetched, first, *unread):
    virt_count = own_t.shape[0]
    width, share = flat.shape[1], fetched.shape[1]
    unit = width // 8

    def body(own_ref, far_ref, flat_ref, fetched_ref, *out_refs):
        shift = jnp.where(near_place() == 1, width // 2, 0)
        for n, out_ref in enumerate(out_refs):
            source = pl.multiple_of(lax.rem(first + n * unit + shift, width), unit)
            total = dot_rows(own_ref[...], flat_ref[:, pl.ds(source, unit)])
            total += dot_rows(far_ref[...], fetched_ref[:, n * unit : (n + 1) * unit])
            out_ref[...] = total.astype(BF16)

    out = [shaped((virt_count, unit))] * (share // unit)
    return kernel(body, "partial_integrals", 12, out, (own_t, far_t, flat, fetched), unread)


def amplitude_bands(rows_ref, columns_ref, first, part_refs, other_refs, out_ref):
    virt_count, unit = part_refs[0].shape
    block = 32

    for n, (part_ref, other_ref) in enumerate(zip(part_refs, other_refs, strict=True)):
        at = slice(n * unit, (n + 1) * unit)
        column = jnp.broadcast_to(columns_ref[:, first + n * unit : first + (n + 1) * unit], (8, unit))

        @pl.loop(0, virt_count // block, unroll=8)
        def _(r, at=at, column=column, part_ref=part_ref, other_ref=other_ref):
            band = pl.ds(pl.multiple_of(r * block, block), block)
            divisor = jnp.concatenate([rows_ref[band, :]] * (unit // LANES), axis=1)
            divisor = divisor + jnp.concatenate([column] * (block // 8), axis=0)
            integrals = part_ref[band, :].astype(F32) + other_ref[band, :].astype(F32)
            inverse = pl.reciprocal(divisor, approx=True)
            inverse = inverse * (divisor * inverse - 2.0)
            out_ref[band, at] = (integrals * inverse).astype(BF16)


def amplitude_piece(rows, columns, first, parts, others, *unread):
    count = len(parts)
    virt_count, unit = parts[0].shape

    def body(rows_ref, columns_ref, *refs):
        amplitude_bands(rows_ref, columns_ref, first, refs[:count], refs[count:-1], refs[-1])

    out = shaped((virt_count, count * unit))
    return kernel(body, "amplitude_piece", 12, out, (rows, columns, *parts, *others), unread)


def clip_spans(spans, low, high):
    found = []
    for n, (first, last) in enumerate(spans):
        a, b = max(first, low), min(last, high)
        if a < b:
            found.append((n, a - first, a - low, b - low))
    return found


def own_amplitudes(amps, spans, virt_count, *unread):
    half, unit = virt_count // 2, virt_count // 4

    def body(*refs):
        for core in range(2):

            @pl.when(core_place() == core)
            def _():
                for n, skip, a, b in clip_spans(spans, core * half, (core + 1) * half):
                    for r in range(0, virt_count, unit):
                        refs[-1][a:b, r : r + unit] = refs[n][r : r + unit, skip : skip + b - a].T

    return kernel(body, "own_amplitudes", 12, shaped((half, virt_count)), tuple(amps), unread)


def add_terms(total, own_ref, amp_refs, found, at, unit):
    for n, skip, a, b in found:
        total = total - dot_columns(own_ref[:, a:b], amp_refs[n][at : at + unit, skip : skip + b - a])
    for n, skip, a, b in found:
        if a <= at < b:
            rows = own_ref[...]
            total = total + dot_rows(rows + rows, amp_refs[n][:, skip + at - a : skip + at - a + unit])
    return total


def density_terms(own, amps, found, dtype, *unread):
    aux_rows, virt_count = own.shape
    unit = virt_count // 4

    def body(own_ref, *refs):
        for at in range(0, virt_count, unit):
            total = add_terms(jnp.zeros((aux_rows, unit), F32), own_ref, refs[:-1], found, at, unit)
            refs[-1][:, at : at + unit] = total.astype(dtype)

    return kernel(body, "density_terms", 16, shaped((aux_rows, virt_count), dtype), (own, *amps), unread)


def finish(rows, columns, first, parts, others, own, earlier, near_density):
    count = len(parts)
    virt_count, unit = parts[0].shape
    aux_rows, share = own.shape[0], count * unit
    block = aux_rows // 2
    found = [(0, 0, virt_count - share, virt_count)]

    def body(rows_ref, columns_ref, *refs):
        part_refs, other_refs = refs[:count], refs[count : 2 * count]
        own_ref, earlier_ref, ready_ref, out_ref, amp_ref, density_ref = refs[2 * count :]
        step = pl.program_id(0)

        @pl.when(step == 0)
        def _():
            amplitude_bands(rows_ref, columns_ref, first, part_refs, other_refs, amp_ref)
            for at in range(0, virt_count, unit):
                total = add_terms(earlier_ref[:, at : at + unit], own_ref, [amp_ref], found, at, unit)
                density_ref[:, at : at + unit] = total.astype(BF16)

        band = pl.ds(pl.multiple_of(step * block, block), block)
        density, ready = density_ref[band, :], ready_ref[band, :]
        swap = near_place() == 1
        out_ref[:, 0, :] = jnp.where(swap, density, ready)
        out_ref[:, 1, :] = jnp.where(swap, ready, density)

    return kernel(
        body,
        "finish_density",
        20,
        shaped((aux_rows, 2, virt_count)),
        (rows, columns, *parts, *others, own, earlier, near_density),
        scratch=[pltpu.VMEM((virt_count, share), BF16), pltpu.VMEM((aux_rows, virt_count), BF16)],
        grid=(aux_rows // block,),
        out_specs=pl.BlockSpec((block, 2, virt_count), lambda n: (n, 0, 0)),
    )


def pair_shards(factors, partner, occupied_energy, partner_energy, virtual_energy):
    aux_rows, local_occ, virt_count = factors.shape
    n_aux = lax.axis_size("aux")
    n_occ = lax.axis_size("occ")
    width, unit = local_occ * virt_count, virt_count // 4
    across = [(d, (d + n_aux // 2) % n_aux) for d in range(n_aux)]
    within = [(d, d ^ 1) for d in range(n_aux)]
    def occ_swap(value, k):
        return lax.ppermute(value, "occ", [(d, d ^ k) for d in range(n_occ)])

    far = lax.ppermute(partner, "aux", across)
    flat = factors.reshape(aux_rows, width)
    edges = [n * unit for n in (0, 1, 3, 7, 8)]
    spans = list(zip(edges[:-1], edges[1:], strict=True))
    last = len(spans) - 1
    sent = pick(factors[:, :, :unit].reshape(aux_rows, local_occ * unit), spans[:1])

    line = virtual_energy.reshape(1, virt_count)
    occupied, resident = occupied_energy.reshape(1, local_occ), partner_energy.reshape(1, 1)
    shard, rows, columns = turn(partner, far, occupied, resident, line, sent[0])
    sent += pick(flat, spans[1:], sent[0])
    fetched = [lax.ppermute(piece, "aux", across) for piece in sent]
    by_4 = occ_swap(shard, 4)
    by_2 = occ_swap(shard, 2)
    by_1 = occ_swap(shard, 1)
    by_3 = occ_swap(held(by_2, by_1, fetched[0]), 1)
    by_4 = held(by_4, fetched[1])
    by_7 = occ_swap(by_3, 4)
    by_6 = occ_swap(by_4, 2)
    by_5 = occ_swap(by_4, 1)
    own_t, far_t, own = assemble([shard, by_1, by_2, by_3, by_4, by_5, by_6, by_7])

    def partial(n, *unread):
        return partial_integrals(own_t, far_t, flat, fetched[n], spans[n][0], *unread)

    def other_core(parts):
        return [lax.ppermute(part, "aux", within) for part in parts]

    def amplitudes(n, part, *unread):
        return amplitude_piece(rows, columns, n * unit, [part], other_core([part]), *unread)

    eighths = [(n * unit, (n + 1) * unit) for n in range(8)]
    parts = partial(0)
    parts += partial(1, parts[0])
    amps = [amplitudes(n, part) for n, part in enumerate(parts)]
    parts = partial(2, *amps)
    amps.append(amplitudes(3, parts[0]))
    near_density = density_terms(own, amps, clip_spans(eighths[:4], 0, virt_count), BF16)
    more = [amplitudes(n, part, near_density) for n, part in enumerate(parts[1:], 4)]
    earlier = density_terms(own, more, clip_spans(eighths[4:7], virt_count, width), F32)
    parts = partial(last, earlier)
    others = other_core(parts)
    amp_shard = own_amplitudes(amps, eighths[:4], virt_count, parts[0])
    density = finish(rows, columns, spans[last][0], parts, others, own, earlier, near_density)
    return (amp_shard, density)


def solution(mesh):
    n_aux, n_occ = mesh.shape["aux"], mesh.shape["occ"]
    fetch = n_aux == 2 * 2 and n_occ == 2 * 2 * 2
    return jax.shard_map(
        pair_shards if fetch else scatter_shards,
        mesh=mesh,
        in_specs=(P("aux", "occ", None), P("aux", "occ"), P("occ"), P(), P()),
        out_specs=(P(("occ", "aux"), None), P("aux", "occ", None)),
        check_vma=False,
    )
```
